128 devices in a mesh: dp: 16 (over z_hi, x, core), row: 2 (over z_lo), col: 4 (over y).
Axes of the slice: x: 4, y: 4, z: 4 (z_hi: 2, z_lo: 2; z = z_hi * 2 + z_lo), core: 2. Of those that a mesh axis runs over, the one named last changes fastest.
Arguments:
- block_in: bfloat16 [16384, 1536], P(('dp', 'row'), 'col'), may hold values from -16 to 16
- norm_gain: bfloat16 [1536], P('col'), may hold values from 0.25 to 1.75
- in_weight: bfloat16 [3, 1536, 1536], P(None, 'col', 'row'), may hold values from -0.15625 to 0.15625
- conv_weight: bfloat16 [3, 1536], P(None, ('row', 'col')), may hold values from -3 to 3
- out_weight: bfloat16 [1536, 1536], P('row', 'col'), may hold values from -0.15625 to 0.15625
- ffn_gain: bfloat16 [1536], P('col'), may hold values from 0.25 to 1.75
- gate_up_weight: bfloat16 [2, 1536, 6912], P(None, 'col', 'row'), may hold values from -0.15625 to 0.15625
- down_weight: bfloat16 [6912, 1536], P('row', 'col'), may hold values from -0.15625 to 0.15625
- out_grad: bfloat16 [16384, 1536], P(('dp', 'row'), 'col'), may hold values from -5 to 5
Outputs:
- block_out: bfloat16 [16384, 1536], P(('dp', 'row'), 'col')
- in_grad: bfloat16 [16384, 1536], P(('dp', 'row'), 'col')
- norm_gain_grad: float32 [1536], P('col')
- in_weight_grad: float32 [3, 1536, 1536], P(None, 'col', 'row')
- conv_grad: float32 [3, 1536], P(None, ('row', 'col'))
- out_weight_grad: float32 [1536, 1536], P('row', 'col')
- ffn_gain_grad: float32 [1536], P('col')
- gate_up_grad: float32 [2, 1536, 6912], P(None, 'col', 'row')
- down_grad: float32 [6912, 1536], P('row', 'col')
The draws below stay inside these ranges and needn't reach their ends.
All inputs are finite; a program needn't handle non-finite values.
Results may differ from the reference program's by a relative error of at most 0.0095.
Values may be sent and summed in bfloat16 or wider, within the bound.
No kernel may reach another device: no remote copies, remote signals or barrier semaphores. Data moves between devices by JAX's collectives and lax.ppermute only.
A program may use at most 256 MiB of HBM per device.

```python
import jax
import jax.numpy as jnp
from jax import lax

D = 1536
FF = 6912
KERNEL = 3
LEN = 1024
SEQS = 1
TOKENS = 16384


def draw_block_in(key, part):
    key = jax.random.fold_in(key, 11)
    base_key, row_key = jax.random.split(key, 2)
    position = jnp.arange(D, dtype=jnp.float32) / D
    column_scale = 0.7 * 3.0 ** position
    row_scale = jnp.exp(jax.random.uniform(row_key, (TOKENS, 1), jnp.float32, -0.7, 0.7))
    base = jnp.clip(jax.random.normal(base_key, (TOKENS, D), jnp.float32), -4.0, 4.0)
    return jnp.clip(base * row_scale * column_scale[None, :], -16.0, 16.0).astype(jnp.bfloat16)


def draw_out_grad(key, part):
    key = jax.random.fold_in(key, 23)
    base_key = jax.random.fold_in(key, 0)
    group_size = SEQS * LEN
    place = (jnp.arange(TOKENS) % group_size).astype(jnp.float32) / group_size
    row_scale = (0.6 * 3.0 ** place)[:, None]
    base = jnp.clip(jax.random.normal(base_key, (TOKENS, D), jnp.float32), -4.0, 4.0)
    return jnp.clip(base * row_scale, -5.0, 5.0).astype(jnp.bfloat16)


def levels(rng, shape, cuts, low, largest):
    def one(dim, parts):
        heights = jax.random.uniform(jax.random.fold_in(jax.random.fold_in(rng, 6), dim), (parts,), jnp.float32, low / len(cuts), largest / len(cuts))
        return jnp.repeat(jnp.exp(heights), shape[dim] // parts).reshape((-1,) + (1,) * (len(shape) - dim - 1))

    level = one(*cuts[0])
    for cut in cuts[1:]:
        level = level * one(*cut)
    return level


def scatter_about(key, extent, scale, most, shards=(), kind=jnp.bfloat16):
    drawn = scale * jax.random.normal(key, extent, jnp.float32)
    if shards:
        drawn = drawn * levels(key, extent, shards, -0.22, 0.18)
    return jnp.clip(drawn, -most, most).astype(kind)


def setup_inputs(seed: int = 0) -> dict:
    keys = jax.random.split(jax.random.key(seed), 10)
    block_in = draw_block_in(jax.random.fold_in(keys[9], 71), 0)
    norm_gain = jnp.clip(1.0 + 0.15 * jax.random.normal(keys[1], (D,), jnp.float32), 0.25, 1.75).astype(jnp.bfloat16)
    in_weight = scatter_about(keys[2], (3, D, D), D ** -0.5, 0.15625, ((1, 4), (2, 2)))
    conv_weight = scatter_about(keys[3], (KERNEL, D), 0.45, 3.0, ((1, 8),))
    out_weight = scatter_about(keys[4], (D, D), D ** -0.5, 0.15625, ((0, 2), (1, 4)))
    ffn_gain = jnp.clip(1.0 + 0.15 * jax.random.normal(keys[5], (D,), jnp.float32), 0.25, 1.75).astype(jnp.bfloat16)
    gate_up_weight = scatter_about(keys[6], (2, D, FF), D ** -0.5, 0.15625, ((1, 4), (2, 2)))
    down_weight = scatter_about(keys[7], (FF, D), (FF // 4) ** -0.5, 0.15625, ((0, 2), (1, 4)))
    out_grad = draw_out_grad(jax.random.fold_in(keys[9], 71), 0)
    return {"block_in": block_in, "norm_gain": norm_gain, "in_weight": in_weight, "conv_weight": conv_weight, "out_weight": out_weight, "ffn_gain": ffn_gain, "gate_up_weight": gate_up_weight, "down_weight": down_weight, "out_grad": out_grad}


EPSILON = 1e-05
PRECISE = lax.Precision.HIGHEST

@jax.custom_vjp
def low(v):
    return lax.optimization_barrier(v.astype(jnp.bfloat16)).astype(jnp.float32)

@jax.custom_vjp
def low_back(v):
    return v

def low_keep(v):
    return (low(v), None)

def low_pass(kept, grad):
    return (grad,)

def back_keep(v):
    return (v, None)

def back_low(kept, grad):
    return (low(grad),)
low.defvjp(low_keep, low_pass)
low_back.defvjp(back_keep, back_low)

def rms_normed(inputs, gain_vec):
    inv_rms = lax.rsqrt(lax.optimization_barrier(jnp.mean(inputs * inputs, axis=-1, keepdims=True)) + EPSILON)
    return inputs * inv_rms * gain_vec

def causal_conv(signal, kernel):
    running = kernel[0] * signal
    for lag in range(1, KERNEL):
        running = running + kernel[lag] * jnp.pad(signal[:LEN - lag], ((lag, 0), (0, 0)))
    return running

def forward_pass(inputs, params):
    norm_gain, in_weight, conv_weight, out_weight, ffn_gain, gate_up_weight, down_weight = params
    normed_one = low(rms_normed(inputs, norm_gain))
    projected = low_back(jnp.einsum('td,jde->jte', normed_one, in_weight, precision=PRECISE))
    convolved = causal_conv(projected[0] * projected[2], conv_weight)
    mixer_act = low(projected[1] * convolved)
    stream = inputs + low_back(jnp.dot(mixer_act, out_weight, precision=PRECISE))
    normed_two = low(rms_normed(stream, ffn_gain))
    gate_up = low_back(jnp.einsum('td,jde->jte', normed_two, gate_up_weight, precision=PRECISE))
    hidden = low(jax.nn.silu(gate_up[0]) * gate_up[1])
    return stream + low_back(jnp.dot(hidden, down_weight, precision=PRECISE))

def reference(block_in, norm_gain, in_weight, conv_weight, out_weight, ffn_gain, gate_up_weight, down_weight, out_grad):
    params = tuple((weight.astype(jnp.float32) for weight in (norm_gain, in_weight, conv_weight, out_weight, ffn_gain, gate_up_weight, down_weight)))
    seq_inputs = block_in.astype(jnp.float32).reshape(TOKENS // LEN, LEN, D)
    seq_grads = out_grad.astype(jnp.float32).reshape(TOKENS // LEN, LEN, D)

    def seq_step(totals, seq_item):
        seq_out, pullback = jax.vjp(forward_pass, seq_item[0], params)
        input_grad, param_grads = pullback(seq_item[1])
        return (jax.tree.map(jnp.add, totals, param_grads), (seq_out, input_grad))
    zero_grads = tuple((jnp.zeros(weight.shape, jnp.float32) for weight in params))
    grads_sum, (outputs, input_grads) = lax.scan(seq_step, zero_grads, (seq_inputs, seq_grads))
    return (outputs.reshape(TOKENS, D).astype(jnp.bfloat16), input_grads.reshape(TOKENS, D).astype(jnp.bfloat16), grads_sum[0], grads_sum[1], grads_sum[2], grads_sum[3], grads_sum[4], grads_sum[5], grads_sum[6])
```

```python
import jax
import jax.numpy as jnp
from jax import lax
from jax.sharding import Mesh, PartitionSpec as P

D = 1536
LEN = 1024
EPSILON = 1e-05
FB = 896
FSTARTS = (0, 896, 1792, 2560)

bf16 = jnp.bfloat16
f32 = jnp.float32


def yshift(v, d):
    return lax.ppermute(v, "y", [(i, (i + d) % 4) for i in range(4)])


def xshift(v, d):
    return lax.ppermute(v, "x", [(i, (i + d) % 4) for i in range(4)])


def zshift(v, d):
    return lax.ppermute(v, ("zh", "zl"), [(i, (i + d) % 4) for i in range(4)])


def kswap(v):
    return lax.ppermute(v, "k", [(0, 1), (1, 0)])


def ygather(v):
    two = yshift(v, 2)
    return [v, yshift(v, 3), two, yshift(v, 1)]


def yexchange(block_for):
    two = yshift(block_for(2), 2)
    one = yshift(block_for(1), 1)
    three = yshift(block_for(3), 3)
    return [block_for(0), three, two, one]


def yreduce(pieces):
    got = yexchange(lambda j: pieces[j].astype(bf16) if j else pieces[0])
    return got[0].astype(f32) + got[1].astype(f32) + got[2].astype(f32) + got[3].astype(f32)


def zexchange(v):
    half = v.shape[0] // 2
    up = zshift(v[:half], 1)
    down = zshift(v[half:], 3)
    return jnp.concatenate([up, down], axis=0)


def pick(stacked, index):
    return lax.dynamic_index_in_dim(stacked, index, 0, keepdims=False)


def dot(a, b):
    return jnp.dot(a, b, preferred_element_type=f32)


def dot_t(a, b):
    return lax.dot_general(a, b, (((1,), (1,)), ((), ())), preferred_element_type=f32)


def t_dot(a, b):
    return lax.dot_general(a, b, (((0,), (0,)), ((), ())), preferred_element_type=f32)


def both(k, mine, other, axis):
    return jnp.where(
        k == 0,
        jnp.concatenate([mine, other], axis=axis),
        jnp.concatenate([other, mine], axis=axis),
    )


def fetch_in(weight, k, y):
    rows = lax.dynamic_slice_in_dim(weight, k * 192, 192, axis=1)
    blocks = jnp.stack([rows[:, :, 192 * b : 192 * b + 192] for b in range(4)])
    own = jnp.stack(yexchange(lambda j: pick(blocks, (y + j) % 4)))
    other = zexchange(own)
    halves = jnp.stack([own, other])
    swapped = kswap(halves)
    full = both(k, halves, swapped, 3)
    return [full[r].transpose(0, 2, 1, 3).reshape(D, 3 * 192) for r in range(2)]


def fetch_out(weight, k, y):
    rows = lax.dynamic_slice_in_dim(weight, k * 384, 384, axis=0)
    own = jnp.stack(ygather(rows))
    other = zexchange(own)
    halves = jnp.stack([own, other])
    full = both(k, halves, kswap(halves), 2)
    full = full.transpose(2, 0, 1, 3).reshape(4, 192, 2, D)
    full = jnp.concatenate([full, full], axis=0)
    full = lax.dynamic_slice_in_dim(full, y, 4, axis=0)
    return full.transpose(0, 2, 1, 3).reshape(D, D)


def fetch_gate_up(weight, x, k, y):
    rows = lax.dynamic_slice(weight, (k, x * 96, 0), (1, 96, 3456))[0]
    blocks = jnp.stack([rows[:, s : s + FB] for s in FSTARTS])
    part = jnp.stack(yexchange(lambda j: pick(blocks, (y + j) % 4)))
    own = lax.all_gather(part, "x")
    other = zexchange(own)
    result = []
    for half in (own, other):
        theirs = kswap(half)
        result.append([v.transpose(1, 0, 2, 3).reshape(D, FB) for v in (half, theirs)])
    return result


def fetch_down(weight, x, k, y):
    blocks = jnp.stack([weight[s : s + FB] for s in FSTARTS])
    blocks = blocks.reshape(4, 8, 112, 384)
    blocks = lax.dynamic_index_in_dim(blocks, x * 2 + k, 1, keepdims=False)
    part = jnp.stack(yexchange(lambda j: pick(blocks, (y + j) % 4)))
    own = lax.all_gather(part, "x")
    other = zexchange(own)
    keep = (y < 3) | (jnp.arange(FB) >= 128)
    result = []
    for half in (own, other):
        full = both(k, half[:, :, None], kswap(half)[:, :, None], 2)
        full = full.transpose(0, 2, 3, 1, 4).reshape(FB, D)
        result.append(jnp.where(keep[:, None], full, 0))
    return result


def sum_over_x(pieces_of, x):
    got = [pieces_of(x).astype(f32)]
    for d in (2, 1, 3):
        got.append(xshift(pieces_of((x + d) % 4).astype(bf16), d).astype(f32))
    return got[0] + got[1] + got[2] + got[3]


def sum_over_z(own, other, zh, zl):
    z = 2 * zh + zl
    total = pick(own, zh).astype(f32)
    total = total + zshift(pick(own, 1 - zh).astype(bf16), 2).astype(f32)
    for d in (1, 3):
        total = total + zshift(pick(other, ((z + d) % 4) // 2).astype(bf16), d).astype(f32)
    return total


def to_columns(blocks, y):
    got = jnp.stack(yexchange(lambda j: blocks[j].astype(bf16)))
    return [pick(got, (b - y) % 4) for b in range(4)]


def reduce_gate_up(mine, theirs, zh, x, k, zl, y):
    total = mine + kswap(theirs.astype(bf16)).astype(f32)
    total = total.reshape(4, 4, 96, 2 * FB)
    total = sum_over_x(lambda i: lax.dynamic_index_in_dim(total, i, 1, keepdims=False), x)
    total = total.reshape(4, 2, 48, 2 * FB).swapaxes(0, 1)
    total = sum_over_z(total[..., :FB], total[..., FB:], zh, zl)
    cols = to_columns(total, y)
    part = jnp.concatenate(cols[:3] + [cols[3][:, 128:]], axis=1)
    full = lax.all_gather(part, ("k", "x", "zh"), axis=0, tiled=True)
    return full.reshape(2, 384, 3456).astype(f32)


def reduce_rows(own, other, zh, x, k, zl, y):
    rows = own.shape[0] // 16
    both_r = jnp.stack([own, other]).reshape(2, 2, 8 * rows, D)
    total = lax.dynamic_index_in_dim(both_r, k, 1, keepdims=False) + kswap(
        lax.dynamic_index_in_dim(both_r, 1 - k, 1, keepdims=False).astype(bf16)
    ).astype(f32)
    total = total.reshape(2, 4, 2 * rows, D)
    total = sum_over_x(lambda i: lax.dynamic_index_in_dim(total, i, 1, keepdims=False), x)
    total = total.reshape(2, 2, rows, D)
    total = sum_over_z(total[0], total[1], zh, zl)
    cols = to_columns([total[:, 384 * j : 384 * j + 384] for j in range(4)], y)
    full = lax.all_gather(jnp.stack(cols), ("k", "x", "zh"))
    full = full.transpose(1, 0, 2, 3).reshape(4, 16 * rows, 384)
    return full.astype(f32)


def reduce_in(own, other, zh, x, k, zl, y):
    both_r = jnp.stack([own, other]).reshape(2, 4, 2, 192, 576)
    total = lax.dynamic_index_in_dim(both_r, k, 2, keepdims=False) + kswap(
        lax.dynamic_index_in_dim(both_r, 1 - k, 2, keepdims=False).astype(bf16)
    ).astype(f32)
    total = total.reshape(2, 4, 4, 48, 576)
    total = sum_over_x(lambda i: lax.dynamic_index_in_dim(total, i, 2, keepdims=False), x)
    total = total.reshape(2, 4, 2, 24, 576).transpose(0, 2, 1, 3, 4)
    total = sum_over_z(total[0], total[1], zh, zl)
    cols = to_columns(total, y)
    part = jnp.stack(cols, axis=1)
    part = part.reshape(24, 4, 3, 192).transpose(2, 0, 1, 3).reshape(3, 24, 768)
    full = lax.all_gather(part, ("k", "x", "zh"))
    return full.transpose(1, 0, 2, 3).reshape(3, 384, 768).astype(f32)


def row_sum(v):
    return jnp.sum(v, axis=1, keepdims=True)


def body(
    block_in,
    norm_gain,
    in_weight,
    conv_weight,
    out_weight,
    ffn_gain,
    gate_up_weight,
    down_weight,
    out_grad,
):
    zh = lax.axis_index("zh")
    x = lax.axis_index("x")
    k = lax.axis_index("k")
    zl = lax.axis_index("zl")
    y = lax.axis_index("y")

    sent = jnp.concatenate(
        [block_in, norm_gain[None], ffn_gain[None], jnp.zeros((14, 384), bf16)], axis=0
    )
    gathered = jnp.concatenate(ygather(sent), axis=1)
    tokens = gathered[:512]
    gain_one = gathered[512].astype(f32)
    gain_two = gathered[513].astype(f32)
    tail = lax.ppermute(tokens[496:], "zl", [(0, 1)])
    taps_other = lax.ppermute(conv_weight, "zl", [(0, 1), (1, 0)])

    w_in = fetch_in(in_weight, k, y)
    w_out = fetch_out(out_weight, k, y)
    w_gate_up = fetch_gate_up(gate_up_weight, x, k, y)
    w_down = fetch_down(down_weight, x, k, y)

    def norm_one(values):
        wide = values.astype(f32)
        inv = lax.rsqrt(row_sum(wide * wide) / D + EPSILON)
        hat = wide * inv
        return inv, hat, (hat * gain_one).astype(bf16)

    inv_one, hat_one, normed_one = norm_one(tokens)
    _, _, normed_tail = norm_one(tail)

    parts = []
    acts = []
    taps_both = [conv_weight.astype(f32), taps_other.astype(f32)]
    for r in range(2):
        proj = dot(normed_one, w_in[r])
        proj_tail = dot(normed_tail, w_in[r])
        b_part, c_part, x_part = (proj[:, 192 * i : 192 * i + 192] for i in range(3))
        before = proj_tail[8:, :192] * proj_tail[8:, 384:]
        mixed = jnp.concatenate([before, b_part * x_part], axis=0)
        taps = taps_both[r]
        conv = (
            taps[0] * mixed[8:520] + taps[1] * mixed[7:519] + taps[2] * mixed[6:518]
        )
        acts.append((c_part * conv).astype(bf16))
        parts.append((b_part, c_part, x_part, mixed, conv))

    act = jnp.concatenate(acts, axis=1)
    act_all = jnp.concatenate(ygather(act), axis=1)
    stream = tokens.astype(f32) + dot(act_all, w_out)
    inv_two = lax.rsqrt(row_sum(stream * stream) / D + EPSILON)
    hat_two = stream * inv_two
    normed_two = (hat_two * gain_two).astype(bf16)

    grads_all = jnp.concatenate(ygather(out_grad), axis=1)

    hidden = []
    back = []
    for r in range(2):
        first = dot(normed_two, w_gate_up[r][0])
        second = dot(normed_two, w_gate_up[r][1])
        gate = jnp.where(k == 0, first, second)
        up = jnp.where(k == 0, second, first)
        sig = jax.nn.sigmoid(gate)
        silu = gate * sig
        hidden.append((silu * up).astype(bf16))
        hidden_grad = dot_t(grads_all, w_down[r])
        gate_back = (hidden_grad * up * sig * (1.0 + gate * (1.0 - sig))).astype(bf16)
        up_back = (hidden_grad * silu).astype(bf16)
        back.append(
            (jnp.where(k == 0, gate_back, up_back), jnp.where(k == 0, up_back, gate_back))
        )

    hidden_all = jnp.concatenate(hidden, axis=1)
    down_all = jnp.concatenate(w_down, axis=0)
    out_parts = dot(hidden_all, down_all)
    out_sum = yreduce([out_parts[:, 384 * j : 384 * j + 384] for j in range(4)])
    block_out = (stream[:, :384] + out_sum).astype(bf16)

    back_mine = jnp.concatenate([back[0][0], back[1][0]], axis=1)
    back_theirs = jnp.concatenate([back[0][1], back[1][1]], axis=1)
    back_all = jnp.concatenate([back_mine, back_theirs], axis=1)
    w_back = jnp.concatenate(
        [w_gate_up[0][0], w_gate_up[1][0], w_gate_up[0][1], w_gate_up[1][1]], axis=1
    )
    two_parts = [
        dot_t(back_all, w_back[384 * j : 384 * j + 384]) for j in range(4)
    ]
    two_grad = yreduce(two_parts)
    two_all = ygather(two_grad.astype(bf16))
    two_all = jnp.concatenate(two_all, axis=1).astype(f32)

    down_grad = t_dot(hidden_all, grads_all)
    down_grad = reduce_rows(down_grad[:FB], down_grad[FB:], zh, x, k, zl, y)
    down_grad = jnp.concatenate(
        [down_grad[0], down_grad[1], down_grad[2], down_grad[3][128:]], axis=0
    )
    gate_up_grad = reduce_gate_up(
        t_dot(normed_two, back_mine), t_dot(normed_two, back_theirs), zh, x, k, zl, y
    )

    weighted_two = gain_two * two_all
    mean_two = row_sum(weighted_two * hat_two) / D
    stream_grad = grads_all.astype(f32) + inv_two * (weighted_two - hat_two * mean_two)
    stream_back = stream_grad.astype(bf16)
    own_weighted = gain_two[:384] * two_grad
    own_stream_grad = out_grad.astype(f32) + inv_two * (
        own_weighted - hat_two[:, :384] * mean_two
    )
    gain_two_part = jnp.sum(two_grad * hat_two[:, :384], axis=0)

    mixer_grad = dot_t(stream_back, w_out[:384])
    out_weight_grad = t_dot(act, stream_back)
    conv_parts = []
    proj_back = []
    grads = [mixer_grad[:, 192 * r : 192 * r + 192] for r in range(2)]
    conv_backs = [grads[r] * parts[r][1] for r in range(2)]
    after_both = lax.ppermute(
        jnp.concatenate([conv_backs[1][:8], conv_backs[0][:8]], axis=1), "zl", [(1, 0)]
    )
    for r in range(2):
        b_part, c_part, x_part, mixed, conv = parts[r]
        taps = taps_both[r]
        grad = grads[r]
        conv_back = conv_backs[r]
        after = after_both[:, 192 * r : 192 * r + 192]
        longer = jnp.concatenate([conv_back, after], axis=0)
        mixed_grad = (
            taps[0] * conv_back + taps[1] * longer[1:513] + taps[2] * longer[2:514]
        )
        conv_parts.append(
            jnp.stack(
                [jnp.sum(conv_back * mixed[8 - lag : 520 - lag], axis=0) for lag in range(3)]
            )
        )
        proj_back.append(
            jnp.concatenate([mixed_grad * x_part, grad * conv, mixed_grad * b_part], axis=1).astype(
                bf16
            )
        )
    proj_all = jnp.concatenate(proj_back, axis=1)
    w_in_all = jnp.concatenate(w_in, axis=1)
    one_part = dot_t(proj_all, w_in_all)
    inner_one = lax.psum(jnp.sum(one_part * gain_one * hat_one, axis=1), "y")
    one_grad = yreduce([one_part[:, 384 * j : 384 * j + 384] for j in range(4)])
    in_own = t_dot(normed_one, proj_back[0])
    in_other = t_dot(normed_one, proj_back[1])
    in_weight_grad = reduce_in(in_own, in_other, zh, x, k, zl, y)
    out_weight_grad = reduce_rows(
        out_weight_grad[:192], out_weight_grad[192:], zh, x, k, zl, y
    ).reshape(768, 384)

    own_hat = hat_one[:, :384]
    gain_one_part = jnp.sum(one_grad * own_hat, axis=0)
    in_grad = own_stream_grad + inv_one * (
        gain_one[:384] * one_grad - own_hat * (inner_one / D)[:, None]
    )
    in_grad = in_grad.astype(bf16)

    conv_other = zshift_pair(conv_parts[1])
    small = jnp.concatenate(
        [
            (conv_parts[0] + conv_other).reshape(-1),
        ]
    )
    conv_grad = lax.psum(small, ("zh", "x", "k")).reshape(3, 192)
    gains = lax.psum(jnp.stack([gain_one_part, gain_two_part]), ("zh", "x", "k", "zl"))
    return (
        block_out,
        in_grad,
        gains[0],
        in_weight_grad,
        conv_grad,
        out_weight_grad,
        gains[1],
        gate_up_grad,
        down_grad,
    )


def zshift_pair(v):
    return lax.ppermute(v, "zl", [(0, 1), (1, 0)])


def solution(mesh):
    devices = mesh.devices.reshape(2, 4, 2, 2, 4)
    grid = Mesh(devices, ("zh", "x", "k", "zl", "y"))
    tokens = P(("zh", "x", "k", "zl"), "y")
    first = P(None, "y", "zl")
    second = P("zl", "y")
    in_specs = (
        tokens,
        P("y"),
        first,
        P(None, ("zl", "y")),
        second,
        P("y"),
        first,
        second,
        tokens,
    )
    out_specs = (
        tokens,
        tokens,
        P("y"),
        first,
        P(None, ("zl", "y")),
        second,
        P("y"),
        first,
        second,
    )
    return jax.shard_map(body, mesh=grid, in_specs=in_specs, out_specs=out_specs, check_vma=False)
```

```python
import functools

import jax
import jax.numpy as jnp
from jax import lax
from jax.experimental import pallas as pl
from jax.experimental.pallas import tpu as pltpu
from jax.sharding import Mesh, PartitionSpec as P

D = 1536
LEN = 1024
EPSILON = 1e-05
FB = 896
FSTARTS = (0, 896, 1792, 2560)

bf16 = jnp.bfloat16
f32 = jnp.float32


def yshift(v, d):
    return lax.ppermute(v, "y", [(i, (i + d) % 4) for i in range(4)])


def xshift(v, d):
    return lax.ppermute(v, "x", [(i, (i + d) % 4) for i in range(4)])


def zshift(v, d):
    return lax.ppermute(v, ("zh", "zl"), [(i, (i + d) % 4) for i in range(4)])


def zswap(v):
    return lax.ppermute(v, "zl", [(0, 1), (1, 0)])


def kswap(v):
    return lax.ppermute(v, "k", [(0, 1), (1, 0)])


def ygather(v):
    two = yshift(v, 2)
    return [v, yshift(v, 3), two, yshift(v, 1)]


def yexchange(block_for):
    two = yshift(block_for(2), 2)
    one = yshift(block_for(1), 1)
    three = yshift(block_for(3), 3)
    return [block_for(0), three, two, one]


def yreduce(pieces):
    got = yexchange(lambda j: pieces[j].astype(bf16) if j else pieces[0])
    return got[0].astype(f32) + got[1].astype(f32) + got[2].astype(f32) + got[3].astype(f32)


def zexchange(v):
    half = v.shape[0] // 2
    up = zshift(v[:half], 1)
    down = zshift(v[half:], 3)
    return jnp.concatenate([up, down], axis=0)


def pick(stacked, index):
    return lax.dynamic_index_in_dim(stacked, index, 0, keepdims=False)


def dot(a, b):
    return jnp.dot(a, b, preferred_element_type=f32)


def dot_t(a, b):
    return lax.dot_general(a, b, (((1,), (1,)), ((), ())), preferred_element_type=f32)


def t_dot(a, b):
    return lax.dot_general(a, b, (((0,), (0,)), ((), ())), preferred_element_type=f32)


def after(v, *deps):
    for dep in deps:
        last = lax.slice(dep, [n - 1 for n in dep.shape], dep.shape).reshape(())
        v = v + (last * 0).astype(v.dtype)
    return v


def both(k, mine, other, axis):
    return jnp.where(
        k == 0,
        jnp.concatenate([mine, other], axis=axis),
        jnp.concatenate([other, mine], axis=axis),
    )


def to_owners(blocks, y):
    return jnp.stack(yexchange(lambda j: pick(blocks, (y + j) % 4)))


def pack_mixer(in_weight, out_weight, first):
    rows = lax.dynamic_slice_in_dim(in_weight, first, 48, axis=1)
    turned = lax.dynamic_slice_in_dim(out_weight.T, first, 48, axis=0)
    blocks = []
    for b in range(4):
        cols = slice(192 * b, 192 * b + 192)
        blocks.append(
            jnp.concatenate(
                [
                    rows[0, :, cols],
                    rows[1, :, cols],
                    rows[2, :, cols],
                    jnp.zeros((48, 64), bf16),
                    turned[:, cols],
                ],
                axis=1,
            )
        )
    return jnp.stack(blocks)


def pack_ffn(gate_up_weight, down_weight, first):
    rows = lax.dynamic_slice_in_dim(gate_up_weight, first, 48, axis=1)
    turned = lax.dynamic_slice_in_dim(down_weight.T, first, 48, axis=0)
    blocks = []
    for start in FSTARTS:
        cols = slice(start, start + FB)
        down = turned[:, cols]
        if start % FB:
            down = jnp.concatenate([jnp.zeros((48, 128), bf16), down[:, 128:]], axis=1)
        blocks.append(jnp.concatenate([rows[0, :, cols], rows[1, :, cols], down], axis=1))
    return jnp.stack(blocks)


def x_terms(pieces_of, x):
    got = [pieces_of(x)]
    for d in (2, 1, 3):
        got.append(xshift(pieces_of((x + d) % 4).astype(bf16), d))
    return got


def z_terms(own, other, zh, zl):
    z = 2 * zh + zl
    got = [pick(own, zh)]
    got.append(zshift(pick(own, 1 - zh).astype(bf16), 2))
    for d in (1, 3):
        got.append(zshift(pick(other, ((z + d) % 4) // 2).astype(bf16), d))
    return got


def zh_terms(v, axis, zh):
    mine = lax.dynamic_index_in_dim(v, zh, axis, keepdims=False)
    theirs = lax.dynamic_index_in_dim(v, 1 - zh, axis, keepdims=False).astype(bf16)
    return [mine, lax.ppermute(theirs, "zh", [(0, 1), (1, 0)])]


def total_of(terms):
    total = terms[0].astype(f32)
    for term in terms[1:]:
        total = total + term.astype(f32)
    return total


def to_columns(blocks, y):
    got = jnp.stack(yexchange(lambda j: blocks[j].astype(bf16)))
    return [pick(got, (b - y) % 4) for b in range(4)]


def gather_zh(part, zh):
    other = lax.ppermute(part, "zh", [(0, 1), (1, 0)])
    return jnp.where(zh == 0, jnp.stack([part, other]), jnp.stack([other, part]))


def split_k(v, k, axis):
    mine = lax.dynamic_index_in_dim(v, k, axis, keepdims=False)
    theirs = lax.dynamic_index_in_dim(v, 1 - k, axis, keepdims=False)
    return mine.astype(f32) + kswap(theirs.astype(bf16)).astype(f32)


TILES = ((0, 256), (256, 256), (512, 256), (768, 128))
CHEAP = pl.CostEstimate(flops=1_000_000, bytes_accessed=1_000_000, transcendentals=0)
WIDE = pltpu.CompilerParams(
    dimension_semantics=("arbitrary",), vmem_limit_bytes=50 * 1024 * 1024
)


def load_mixer(source, rows, sems):
    copies = []
    for r in range(2):
        for b in range(4):
            for e in range(8):
                first = 384 * b + 48 * e
                copies.append(
                    pltpu.make_async_copy(
                        source.at[e, r, b],
                        rows.at[r, pl.ds(first, 48)],
                        sems.at[32 * r + 8 * b + e],
                    )
                )
    for copy in copies:
        copy.start()
    for copy in copies:
        copy.wait()


def mixer_kernel(
    half_ref, x0, x1, x2, x3, swap_ref, taps_ref, w_hbm, n_ref, inv_ref, proj0, proj1,
    conv0, conv1, before0, before1, act0, act1, wo0, wo1, p0, p1, p2, p3, w_ref, sems,
):
    load_mixer(w_hbm, w_ref, sems)
    xs = (x0, x1, x2, x3)
    gain = jnp.concatenate([ref[512:528, :] for ref in xs], axis=1)[:1].astype(f32)
    for i in range(4):
        rows = pl.ds(128 * i, 128)
        wide = jnp.concatenate([ref[rows, :] for ref in xs], axis=1).astype(f32)
        inv = lax.rsqrt(jnp.sum(wide * wide, axis=1, keepdims=True) / D + EPSILON)
        inv_ref[rows, :] = inv
        n_ref[rows, :] = (wide * inv * gain).astype(bf16)
    tail = swap_ref[:16, :].astype(f32)
    tail = jnp.where(half_ref[0] == 1, tail, 0.0)
    inv = lax.rsqrt(jnp.sum(tail * tail, axis=1, keepdims=True) / D + EPSILON)
    n_tail = (tail * inv * gain).astype(bf16)
    own_taps = taps_ref[...].astype(f32)
    other_taps = swap_ref[16:32, :192].astype(f32)
    line = lax.broadcasted_iota(jnp.int32, (512, 192), 0)
    acts = (act0, act1)
    for r, taps in ((0, own_taps), (1, other_taps)):
        proj_ref = (proj0, proj1)[r]
        proj_ref[...] = dot(n_ref[...], w_ref[r, :, :576])
        proj_tail = dot(n_tail, w_ref[r, :, :576])
        before = proj_tail[8:, :192] * proj_tail[8:, 384:]
        (before0, before1)[r][...] = before
        mixed = proj_ref[:, :192] * proj_ref[:, 384:576]
        one = jnp.where(line == 0, before[7:8], pltpu.roll(mixed, 1, 0))
        two = jnp.where(
            line == 0, before[6:7], jnp.where(line == 1, before[7:8], pltpu.roll(mixed, 2, 0))
        )
        conv = taps[0:1] * mixed + taps[1:2] * one + taps[2:3] * two
        (conv0, conv1)[r][...] = conv
        acts[r][...] = (proj_ref[:, 192:384] * conv).astype(bf16)
        (wo0, wo1)[r][...] = w_ref[r, :, 640:]
    for j, ref in enumerate((p0, p1, p2, p3)):
        rows = pl.ds(384 * j, 384)
        part = dot_t(act0[...], wo0[rows, :]) + dot_t(act1[...], wo1[rows, :])
        ref[...] = part.astype(ref.dtype)


def mixer_call(half, pieces, swapped, taps, weight, *deps):
    whole = pl.BlockSpec(memory_space=pltpu.VMEM)

    def kernel(*refs):
        mixer_kernel(*refs[:8], *refs[8 + len(deps) :])

    def shape(*dims, kind=f32):
        return jax.ShapeDtypeStruct(dims, kind)

    return pl.pallas_call(
        kernel,
        in_specs=[pl.BlockSpec(memory_space=pltpu.SMEM)]
        + [whole] * 6
        + [pl.BlockSpec(memory_space=pl.ANY)] * (1 + len(deps)),
        out_specs=[whole] * 16,
        out_shape=[shape(512, D, kind=bf16), shape(512, 1)]
        + [shape(512, 576)] * 2
        + [shape(512, 192)] * 2
        + [shape(8, 192)] * 2
        + [shape(512, 192, kind=bf16)] * 2
        + [shape(D, 192, kind=bf16)] * 2
        + [shape(512, 384)]
        + [shape(512, 384, kind=bf16)] * 3,
        scratch_shapes=[pltpu.VMEM((2, D, 832), bf16), pltpu.SemaphoreType.DMA((64,))],
        compiler_params=pltpu.CompilerParams(vmem_limit_bytes=50 * 1024 * 1024),
        cost_estimate=CHEAP,
        name="mixer",
    )(half, *pieces, swapped, taps, weight, *deps)


def stream_kernel(*refs):
    q_refs, s_refs, g_refs = refs[:4], refs[4:8], refs[8:12]
    own_ref, gain_ref, wo0, wo1, proj0, proj1 = refs[12:18]
    sb_ref, grad0, grad1, halo_ref, sg_ref, gain_out = refs[-6:]
    gain = gain_ref[...]
    sums = jnp.zeros((1, 384), f32)
    for i in range(4):
        rows = pl.ds(128 * i, 128)
        stream = jnp.concatenate([ref[rows, :] for ref in s_refs], axis=1).astype(f32)
        inv = lax.rsqrt(jnp.sum(stream * stream, axis=1, keepdims=True) / D + EPSILON)
        hat = stream * inv
        weighted = gain * jnp.concatenate([ref[rows, :] for ref in q_refs], axis=1).astype(f32)
        mean = jnp.sum(weighted * hat, axis=1, keepdims=True) / D
        grads = jnp.concatenate([ref[rows, :] for ref in g_refs], axis=1).astype(f32)
        sb_ref[rows, :] = (grads + inv * (weighted - hat * mean)).astype(bf16)
        own = own_ref[rows, :]
        own_hat = hat[:, :384]
        sg_ref[rows, :] = grads[:, :384] + inv * (gain[:, :384] * own - own_hat * mean)
        sums = sums + jnp.sum(own * own_hat, axis=0, keepdims=True)
    gain_out[...] = sums
    for r in range(2):
        grad_ref = (grad0, grad1)[r]
        grad_ref[...] = dot(sb_ref[...], (wo0, wo1)[r][...])
        halo_ref[1 - r] = grad_ref[:8, :] * (proj0, proj1)[r][:8, 192:384]


def stream_call(two_all, streams, grads, two_grad, gain, w_out, proj, *deps):
    whole = pl.BlockSpec(memory_space=pltpu.VMEM)
    return pl.pallas_call(
        stream_kernel,
        in_specs=[whole] * 18 + [pl.BlockSpec(memory_space=pl.ANY)] * len(deps),
        out_specs=[whole] * 6,
        out_shape=[
            jax.ShapeDtypeStruct((512, D), bf16),
            jax.ShapeDtypeStruct((512, 192), f32),
            jax.ShapeDtypeStruct((512, 192), f32),
            jax.ShapeDtypeStruct((2, 8, 192), f32),
            jax.ShapeDtypeStruct((512, 384), f32),
            jax.ShapeDtypeStruct((1, 384), f32),
        ],
        compiler_params=pltpu.CompilerParams(vmem_limit_bytes=50 * 1024 * 1024),
        cost_estimate=CHEAP,
        name="stream",
    )(*two_all, *streams, *grads, two_grad, gain, *w_out, *proj, *deps)


def back_kernel(
    x0, x1, x2, x3, grad0, grad1, proj0, proj1, conv0, conv1, before0, before1, halo_ref,
    swap_ref, taps_ref, w_hbm, pb0, pb1, p0, p1, p2, p3, gain_out, taps0, taps1, w_ref, sems,
):
    load_mixer(w_hbm, w_ref, sems)
    xs = (x0, x1, x2, x3)
    own_taps = taps_ref[...].astype(f32)
    other_taps = swap_ref[16:32, :192].astype(f32)
    line = lax.broadcasted_iota(jnp.int32, (512, 192), 0)
    for r, taps in ((0, own_taps), (1, other_taps)):
        grad_ref, proj_ref = (grad0, grad1)[r], (proj0, proj1)[r]
        before, halo = (before0, before1)[r][...], halo_ref[r]
        grad = grad_ref[...]
        b_part = proj_ref[:, :192]
        x_part = proj_ref[:, 384:576]
        conv_back = grad * proj_ref[:, 192:384]
        one = jnp.where(line == 511, halo[0:1], pltpu.roll(conv_back, 511, 0))
        two = jnp.where(
            line == 510,
            halo[0:1],
            jnp.where(line == 511, halo[1:2], pltpu.roll(conv_back, 510, 0)),
        )
        mixed_grad = taps[0:1] * conv_back + taps[1:2] * one + taps[2:3] * two
        (pb0, pb1)[r][...] = jnp.concatenate(
            [
                mixed_grad * x_part,
                grad * (conv0, conv1)[r][...],
                mixed_grad * b_part,
                jnp.zeros((512, 64), f32),
            ],
            axis=1,
        ).astype(bf16)
        mixed = b_part * x_part
        lag_one = jnp.where(line == 0, before[7:8], pltpu.roll(mixed, 1, 0))
        lag_two = jnp.where(
            line == 0, before[6:7], jnp.where(line == 1, before[7:8], pltpu.roll(mixed, 2, 0))
        )
        (taps0, taps1)[r][...] = jnp.concatenate(
            [
                jnp.sum(conv_back * lagged, axis=0, keepdims=True)
                for lagged in (mixed, lag_one, lag_two)
            ],
            axis=0,
        )
    gain = jnp.concatenate([ref[512:528, :] for ref in xs], axis=1)[:1].astype(f32)
    ones = jnp.ones((8, D), bf16)
    inner = []
    sums = jnp.zeros((1, D), f32)
    for i in range(4):
        rows = pl.ds(128 * i, 128)
        part = dot_t(pb0[rows, :576], w_ref[0, :, :576]) + dot_t(
            pb1[rows, :576], w_ref[1, :, :576]
        )
        for j, ref in enumerate((p0, p1, p2, p3)):
            ref[rows, :] = part[:, 384 * j : 384 * j + 384].astype(ref.dtype)
        wide = jnp.concatenate([ref[rows, :] for ref in xs], axis=1).astype(f32)
        inv = lax.rsqrt(jnp.sum(wide * wide, axis=1, keepdims=True) / D + EPSILON)
        product = part * (wide * inv)
        sums = sums + jnp.sum(product, axis=0, keepdims=True)
        product = product * gain
        high = product.astype(bf16)
        low = (product - high.astype(f32)).astype(bf16)
        inner.append(dot_t(ones, high) + dot_t(ones, low))
    gain_out[...] = sums
    empty = jnp.zeros((1, 256), f32)
    rows = []
    total = jnp.concatenate(inner, axis=1)[:1]
    high = total.astype(bf16).astype(f32)
    for term in (high, total - high):
        rows.append(term[:, :384])
        rows.append(jnp.concatenate([term[:, 384:], empty], axis=1))
    inner_rows = jnp.concatenate(rows + [jnp.zeros((12, 384), f32)], axis=0)
    for ref in (p0, p1, p2, p3):
        ref[512:528, :] = inner_rows.astype(ref.dtype)


def back_call(pieces, grads, proj, conv, before, halo, swapped, taps, weight, *deps):
    whole = pl.BlockSpec(memory_space=pltpu.VMEM)

    def kernel(*refs):
        back_kernel(*refs[:16], *refs[16 + len(deps) :])

    return pl.pallas_call(
        kernel,
        in_specs=[whole] * 15 + [pl.BlockSpec(memory_space=pl.ANY)] * (1 + len(deps)),
        out_specs=[whole] * 9,
        out_shape=[jax.ShapeDtypeStruct((512, 640), bf16)] * 2
        + [jax.ShapeDtypeStruct((528, 384), f32)]
        + [jax.ShapeDtypeStruct((528, 384), bf16)] * 3
        + [jax.ShapeDtypeStruct((1, D), f32)]
        + [jax.ShapeDtypeStruct((3, 192), f32)] * 2,
        scratch_shapes=[pltpu.VMEM((2, D, 832), bf16), pltpu.SemaphoreType.DMA((64,))],
        compiler_params=pltpu.CompilerParams(vmem_limit_bytes=50 * 1024 * 1024),
        cost_estimate=CHEAP,
        name="back",
    )(*pieces, *grads, *proj, *conv, *before, halo, swapped, taps, weight, *deps)


def ffn_finish(full):
    def kernel(full_ref, gate_ref, down_ref):
        wide = full_ref[...].astype(f32)
        gate_ref[...] = wide[:, :, :48].reshape(2, 384, 384)
        down_ref[...] = wide[:, :, 48:].reshape(384, 384).T

    return pl.pallas_call(
        kernel,
        grid=(9,),
        in_specs=[pl.BlockSpec((8, 2, 72, 384), lambda i: (0, 0, 0, i))],
        out_specs=[
            pl.BlockSpec((2, 384, 384), lambda i: (0, 0, i)),
            pl.BlockSpec((384, 384), lambda i: (i, 0)),
        ],
        out_shape=[
            jax.ShapeDtypeStruct((2, 384, 3456), f32),
            jax.ShapeDtypeStruct((3456, 384), f32),
        ],
        compiler_params=pltpu.CompilerParams(vmem_limit_bytes=50 * 1024 * 1024),
        name="ffn_finish",
    )(full)


def mixer_finish(full, y):
    def kernel(y_ref, full_ref, in_ref, out_ref, own_ref, sum_ref):
        own = jnp.zeros((384, 128), f32)
        total = jnp.zeros((384, 128), f32)
        for b in range(4):
            block = full_ref[:, :, b].astype(f32).reshape(384, FB)
            cols = slice(192 * b, 192 * b + 192)
            for j in range(3):
                in_ref[j, :, cols] = block[:, 192 * j : 192 * j + 192]
            out_ref[cols, :] = block[:, 640:896].T[:192]
            small = block[:, 512:640]
            own = own + jnp.where(y_ref[0] == b, small, 0.0)
            total = total + small
        own_ref[...] = own
        sum_ref[...] = total

    whole = pl.BlockSpec(memory_space=pltpu.VMEM)
    return pl.pallas_call(
        kernel,
        in_specs=[pl.BlockSpec(memory_space=pltpu.SMEM), whole],
        out_specs=[whole] * 4,
        out_shape=[
            jax.ShapeDtypeStruct((3, 384, 768), f32),
            jax.ShapeDtypeStruct((768, 384), f32),
            jax.ShapeDtypeStruct((384, 128), f32),
            jax.ShapeDtypeStruct((384, 128), f32),
        ],
        compiler_params=pltpu.CompilerParams(vmem_limit_bytes=50 * 1024 * 1024),
        name="mixer_finish",
    )(y.astype(jnp.int32)[None], full)


def load_rows(source, rows, sems):
    copies = []
    for b in range(4):
        for e in range(8):
            first = 384 * b + 48 * e
            copies.append(
                pltpu.make_async_copy(
                    source.at[e, b], rows.at[pl.ds(first, 48)], sems.at[8 * b + e]
                )
            )
    for copy in copies:
        copy.start()
    for copy in copies:
        copy.wait()


def ffn_kernel(*refs):
    s_refs, g_refs = refs[:4], refs[4:8]
    gain_ref, w_hbm = refs[8:10]
    n_ref, h_ref, gb_ref, ub_ref = refs[-10:-6]
    p_refs = refs[-6:-2]
    w_ref, sems = refs[-2:]

    @pl.when(pl.program_id(0) == 0)
    def _():
        load_rows(w_hbm, w_ref, sems)

    stream = jnp.concatenate([ref[...] for ref in s_refs], axis=1).astype(f32)
    inv = lax.rsqrt(jnp.sum(stream * stream, axis=1, keepdims=True) / D + EPSILON)
    n_ref[...] = (stream * inv * gain_ref[...]).astype(bf16)
    grads = jnp.concatenate([ref[...] for ref in g_refs], axis=1)
    for first, size in TILES:
        cols = pl.ds(first, size)
        w_pair = jnp.concatenate(
            [w_ref[:, cols], w_ref[:, pl.ds(FB + first, size)]], axis=1
        )
        gate_up = dot(n_ref[...], w_pair)
        gate = gate_up[:, :size]
        up = gate_up[:, size:]
        sig = 1.0 / (1.0 + jnp.exp(-gate))
        silu = gate * sig
        h_ref[:, cols] = (silu * up).astype(bf16)
        hidden_grad = dot(grads, w_ref[:, pl.ds(2 * FB + first, size)])
        gb_ref[:, cols] = (
            hidden_grad * up * sig * (1.0 + gate * (1.0 - sig))
        ).astype(bf16)
        ub_ref[:, cols] = (hidden_grad * silu).astype(bf16)
    back = jnp.concatenate([gb_ref[...], ub_ref[...]], axis=1)
    parts = jnp.concatenate(
        [dot_t(back, w_ref[pl.ds(512 * i, 512), : 2 * FB]) for i in range(3)], axis=1
    )
    for j in range(4):
        p_refs[j][...] = parts[:, 384 * j : 384 * j + 384].astype(p_refs[j].dtype)


def ffn_call(streams, grads, gain, weight, *deps):
    narrow = pl.BlockSpec((256, 384), lambda i: (i, 0))
    middle = pl.BlockSpec((256, FB), lambda i: (i, 0))
    wide = pl.BlockSpec((256, D), lambda i: (i, 0))
    whole = pl.BlockSpec(memory_space=pl.ANY)
    return pl.pallas_call(
        ffn_kernel,
        grid=(2,),
        in_specs=[narrow] * 8
        + [pl.BlockSpec((1, D), lambda i: (0, 0)), whole]
        + [whole] * len(deps),
        out_specs=[wide] + [middle] * 3 + [narrow] * 4,
        out_shape=[jax.ShapeDtypeStruct((512, D), bf16)]
        + [jax.ShapeDtypeStruct((512, FB), bf16)] * 3
        + [jax.ShapeDtypeStruct((512, 384), f32)]
        + [jax.ShapeDtypeStruct((512, 384), bf16)] * 3,
        scratch_shapes=[pltpu.VMEM((D, 3 * FB), bf16), pltpu.SemaphoreType.DMA((32,))],
        compiler_params=WIDE,
        cost_estimate=pl.CostEstimate(
            flops=8_400_000_000, bytes_accessed=16_000_000, transcendentals=500_000
        ),
        name="ffn",
    )(*streams, *grads, gain, weight, *deps)


def block_kernel(place, h0_ref, h1_ref, w_ref, out_ref):
    hidden = jnp.where(pl.program_id(1) < 1, h0_ref[...], h1_ref[...])
    out_ref[0, 0] = dot_t(hidden, w_ref[...].reshape(384, FB)).astype(bf16)


def block_call(own, other, weight, y, *deps):
    def where(j, t, place):
        return ((place[0] + j) % 4, t, 0, 0)

    def kernel(place, h0_ref, h1_ref, w_ref, *rest):
        block_kernel(place, h0_ref, h1_ref, w_ref, rest[-1])

    grid_spec = pltpu.PrefetchScalarGridSpec(
        num_scalar_prefetch=1,
        grid=(4, 2),
        in_specs=[
            pl.BlockSpec((512, FB), lambda j, t, place: (0, 0)),
            pl.BlockSpec((512, FB), lambda j, t, place: (0, 0)),
            pl.BlockSpec((8, None, 48, FB), lambda j, t, place: (0, j, 0, 2)),
        ]
        + [pl.BlockSpec(memory_space=pl.ANY)] * len(deps),
        out_specs=pl.BlockSpec((1, 1, 512, 384), where),
    )
    return pl.pallas_call(
        kernel,
        grid_spec=grid_spec,
        out_shape=jax.ShapeDtypeStruct((4, 2, 512, 384), bf16),
        compiler_params=pltpu.CompilerParams(vmem_limit_bytes=50 * 1024 * 1024),
        cost_estimate=pl.CostEstimate(
            flops=2_800_000_000, bytes_accessed=10_000_000, transcendentals=0
        ),
        name="block",
    )(y.astype(jnp.int32)[None], own, other, weight, *deps)


def row_sum(v):
    return jnp.sum(v, axis=1, keepdims=True)


def body(
    block_in,
    norm_gain,
    in_weight,
    conv_weight,
    out_weight,
    ffn_gain,
    gate_up_weight,
    down_weight,
    out_grad,
):
    zh = lax.axis_index("zh")
    x = lax.axis_index("x")
    k = lax.axis_index("k")
    zl = lax.axis_index("zl")
    y = lax.axis_index("y")

    first = (2 * x + k) * 48
    mixer_own = to_owners(pack_mixer(in_weight, out_weight, first), y)
    sent = jnp.concatenate(
        [block_in, norm_gain[None], ffn_gain[None], jnp.zeros((14, 384), bf16)], axis=0
    )
    sent = ygather(sent)
    gain_one = jnp.concatenate([v[512:513] for v in sent], axis=1).astype(f32)
    gain_two = jnp.concatenate([v[513:514] for v in sent], axis=1).astype(f32)

    swapped = jnp.concatenate(
        [
            jnp.concatenate([v[496:512] for v in sent], axis=1),
            jnp.pad(conv_weight, ((0, 13), (0, D - 192))),
        ],
        axis=0,
    )
    swapped = zswap(swapped)

    mixer_both = jnp.stack([mixer_own, zexchange(mixer_own)])
    w_mixer = lax.all_gather(mixer_both, ("x", "k"))

    blocks = pack_ffn(gate_up_weight, down_weight, first)
    blocks, sent = lax.optimization_barrier((blocks, sent))
    ffn = to_owners(blocks, y)
    ffn, swapped, out_grad_late = lax.optimization_barrier((ffn, swapped, out_grad))
    w_ffn = lax.all_gather(ffn, ("x", "k"))
    grad_pieces = ygather(out_grad_late)
    half = zl.astype(jnp.int32)[None]
    results = mixer_call(half, sent, swapped, conv_weight, w_mixer)
    normed_one, inv_one = results[:2]
    proj, conv, before, acts, w_out = (results[i : i + 2] for i in range(2, 12, 2))

    out_parts, grad_pieces = lax.optimization_barrier((results[12:], grad_pieces))
    stream_own = block_in.astype(f32) + yreduce(out_parts)
    grads_own = jnp.concatenate(grad_pieces, axis=1)
    grads_other = zswap(grads_own)
    stream_sent = stream_own.astype(bf16)
    other = zswap(stream_sent)
    pieces_own = ygather(stream_sent)
    pieces_other = ygather(other)
    other_grads = [grads_other[:, 384 * j : 384 * j + 384] for j in range(4)]
    half_own = ffn_call(pieces_own, grad_pieces, gain_two, w_ffn)
    half_other = ffn_call(pieces_other, other_grads, gain_two, w_ffn, half_own[0])
    own_terms = yexchange(lambda j: half_own[4 + j])
    own_terms, half_other = lax.optimization_barrier((own_terms, half_other))
    other_terms = yexchange(lambda j: half_other[4 + j])
    normed_two = jnp.concatenate([half_own[0], half_other[0]], axis=0)
    theirs = t_dot(
        normed_two,
        jnp.concatenate(
            [jnp.where(k == 0, half[3], half[2]) for half in (half_own, half_other)], axis=0
        ),
    ).astype(bf16)
    block_parts = block_call(half_own[1], half_other[1], w_ffn, y)
    other_terms, half_own, half_other, theirs, block_parts = lax.optimization_barrier(
        (other_terms, half_own, half_other, theirs, block_parts)
    )
    theirs = kswap(theirs)
    sum_other = total_of(other_terms)
    sum_own = total_of(own_terms)
    two_grad = sum_own + zswap(sum_other.astype(bf16)).astype(f32)

    two_all = ygather(two_grad.astype(bf16))

    hidden = jnp.concatenate([half_own[1], half_other[1]], axis=0)
    grads_all = jnp.concatenate([grads_own, grads_other], axis=0)
    mine = t_dot(
        normed_two,
        jnp.concatenate(
            [jnp.where(k == 0, half[2], half[3]) for half in (half_own, half_other)], axis=0
        ),
    )
    gate_up_grad = (mine + theirs.astype(f32)).reshape(4, 4, 2, 48, FB)
    down_grad = t_dot(grads_all, hidden).reshape(4, 2, 192, FB)
    down_grad = split_k(down_grad, k, 1).reshape(4, 4, 2, 24, FB)
    ffn = jnp.concatenate([gate_up_grad, down_grad], axis=3).astype(bf16)
    ffn = jnp.stack([pick(ffn, (b - y) % 4) for b in range(4)])
    ffn, two_all, block_parts = lax.optimization_barrier((ffn, two_all, block_parts))
    block_sum = lax.psum_scatter(block_parts, "y", scatter_dimension=0, tiled=False)
    ffn = ffn.transpose(2, 1, 0, 3, 4).reshape(32, 72, FB)
    ffn = lax.all_to_all(ffn, ("zh", "x", "y"), 0, 0, tiled=True)

    stream_back, *grads, halo, own_stream_grad, gain_two_part = stream_call(
        two_all, pieces_own, grad_pieces, two_grad, gain_two, w_out, proj
    )
    halo = lax.ppermute(halo, "zl", [(1, 0)])
    results = back_call(
        sent, grads, proj, conv, before, halo, swapped, conv_weight, w_mixer
    )
    proj_back = results[:2]
    gain_one_part, *conv_parts = results[6:]
    one_sum = yreduce(results[2:6])
    one_grad = one_sum[:512]
    inner_one = one_sum[512:514].reshape(-1)[:512] + one_sum[514:516].reshape(-1)[:512]
    own_hat = block_in.astype(f32) * inv_one
    in_grad = own_stream_grad + inv_one * (
        gain_one[:, :384] * one_grad - own_hat * (inner_one / D)[:, None]
    )
    in_grad = in_grad.astype(bf16)

    tails = []
    for r in range(2):
        taps_part = conv_parts[r].reshape(-1)
        rest = jnp.concatenate([taps_part[384:], jnp.zeros((192,), f32)])
        small = jnp.stack([gain_two_part[0], taps_part[:384], rest], axis=1)
        small = jnp.pad(small, ((0, D - 384), (577, 60)))
        small = small + jnp.pad(gain_one_part.T, ((0, 0), (576, 63)))
        padded = jnp.pad(acts[r], ((0, 0), (0, 64)))
        tails.append((t_dot(normed_one, proj_back[r]) + small, t_dot(stream_back, padded)))

    def tail_half(index):
        halves = []
        for pair in tails:
            rows = [
                lax.dynamic_index_in_dim(v.reshape(4, 2, 192, -1), index, 1, keepdims=False)
                for v in pair
            ]
            halves.append(jnp.concatenate(rows, axis=2))
        return jnp.stack(halves)

    theirs = tail_half(1 - k)
    theirs, ffn, block_sum = lax.optimization_barrier((theirs, ffn, block_sum))
    block_out = stream_own + total_of([block_sum[0], zswap(block_sum[1])])
    block_out = block_out.astype(bf16)
    mixer = tail_half(k) + kswap(theirs.astype(bf16)).astype(f32)
    cols = list(jnp.sum(ffn.reshape(8, 4, 72, FB).astype(f32), axis=0).astype(bf16))
    part = jnp.concatenate(cols[:3] + [cols[3][:, 128:]], axis=1)
    part = gather_zh(part, zh)
    mixer = jnp.stack([pick(mixer.swapaxes(0, 1), (b - y) % 4) for b in range(4)])
    mixer = jnp.where(zl == 0, mixer, mixer[:, ::-1]).astype(bf16)
    mixer, part = lax.optimization_barrier((mixer, part))
    full = lax.all_gather(part, ("k", "x"))
    gate_up_out, down_out = ffn_finish(full)
    mixer = mixer.reshape(4, 2, 4, 2, 24, FB).transpose(3, 2, 1, 0, 4, 5)
    mixer = lax.all_to_all(
        mixer.reshape(64, 24, FB), ("zh", "x", "zl", "y"), 0, 0, tiled=True
    )
    cols = jnp.sum(mixer.reshape(16, 4, 24, FB).astype(f32), axis=0).astype(bf16)
    part = gather_zh(cols, zh)
    full = lax.all_gather(part, ("k", "x"))
    full, gate_up_out, down_out, in_grad, block_out = lax.optimization_barrier(
        (full, gate_up_out, down_out, in_grad, block_out)
    )
    in_out, out_out, own_small, sum_small = mixer_finish(full, y)
    gain_one_out = sum_small[:, 64]
    gain_two_out = own_small[:, 65]
    conv_out = jnp.concatenate([own_small[:, 66], own_small[:192, 67]]).reshape(3, 192)
    return (
        block_out,
        in_grad,
        gain_one_out,
        in_out,
        conv_out,
        out_out,
        gain_two_out,
        gate_up_out,
        down_out,
    )


def solution(mesh):
    devices = mesh.devices.reshape(2, 4, 2, 2, 4)
    grid = Mesh(devices, ("zh", "x", "k", "zl", "y"))
    tokens = P(("zh", "x", "k", "zl"), "y")
    first = P(None, "y", "zl")
    second = P("zl", "y")
    in_specs = (
        tokens,
        P("y"),
        first,
        P(None, ("zl", "y")),
        second,
        P("y"),
        first,
        second,
        tokens,
    )
    out_specs = (
        tokens,
        tokens,
        P("y"),
        first,
        P(None, ("zl", "y")),
        second,
        P("y"),
        first,
        second,
    )
    return jax.shard_map(body, mesh=grid, in_specs=in_specs, out_specs=out_specs, check_vma=False)
```

```python
import functools

import jax
import jax.numpy as jnp
from jax import lax
from jax.experimental import pallas as pl
from jax.experimental.pallas import tpu as pltpu
from jax.sharding import Mesh, PartitionSpec as P

D = 1536
LEN = 1024
EPSILON = 1e-05
FB = 896
FSTARTS = (0, 896, 1792, 2560)

bf16 = jnp.bfloat16
f32 = jnp.float32


def yshift(v, d):
    return lax.ppermute(v, "y", [(i, (i + d) % 4) for i in range(4)])


def xshift(v, d):
    return lax.ppermute(v, "x", [(i, (i + d) % 4) for i in range(4)])


def zshift(v, d):
    return lax.ppermute(v, ("zh", "zl"), [(i, (i + d) % 4) for i in range(4)])


def zswap(v):
    return lax.ppermute(v, "zl", [(0, 1), (1, 0)])


def kswap(v):
    return lax.ppermute(v, "k", [(0, 1), (1, 0)])


def ygather(v):
    two = yshift(v, 2)
    return [v, yshift(v, 3), two, yshift(v, 1)]


def yexchange(block_for):
    two = yshift(block_for(2), 2)
    one = yshift(block_for(1), 1)
    three = yshift(block_for(3), 3)
    return [block_for(0), three, two, one]


def yreduce(pieces):
    got = yexchange(lambda j: pieces[j].astype(bf16) if j else pieces[0])
    return got[0].astype(f32) + got[1].astype(f32) + got[2].astype(f32) + got[3].astype(f32)


def zexchange(v):
    half = v.shape[0] // 2
    up = zshift(v[:half], 1)
    down = zshift(v[half:], 3)
    return jnp.concatenate([up, down], axis=0)


def pick(stacked, index):
    return lax.dynamic_index_in_dim(stacked, index, 0, keepdims=False)


def dot(a, b):
    return jnp.dot(a, b, preferred_element_type=f32)


def dot_t(a, b):
    return lax.dot_general(a, b, (((1,), (1,)), ((), ())), preferred_element_type=f32)


def t_dot(a, b):
    return lax.dot_general(a, b, (((0,), (0,)), ((), ())), preferred_element_type=f32)


def after(v, *deps):
    for dep in deps:
        last = lax.slice(dep, [n - 1 for n in dep.shape], dep.shape).reshape(())
        v = v + (last * 0).astype(v.dtype)
    return v


def both(k, mine, other, axis):
    return jnp.where(
        k == 0,
        jnp.concatenate([mine, other], axis=axis),
        jnp.concatenate([other, mine], axis=axis),
    )


def to_owners(blocks, y):
    return jnp.stack(yexchange(lambda j: pick(blocks, (y + j) % 4)))


def pack_mixer(in_weight, out_weight, first):
    rows = lax.dynamic_slice_in_dim(in_weight, first, 48, axis=1)
    turned = lax.dynamic_slice_in_dim(out_weight.T, first, 48, axis=0)
    blocks = []
    for b in range(4):
        cols = slice(192 * b, 192 * b + 192)
        blocks.append(
            jnp.concatenate(
                [
                    rows[0, :, cols],
                    rows[1, :, cols],
                    rows[2, :, cols],
                    jnp.zeros((48, 64), bf16),
                    turned[:, cols],
                ],
                axis=1,
            )
        )
    return jnp.stack(blocks)


def pack_ffn(gate_up_weight, down_weight, first):
    rows = lax.dynamic_slice_in_dim(gate_up_weight, first, 48, axis=1)
    turned = lax.dynamic_slice_in_dim(down_weight.T, first, 48, axis=0)
    blocks = []
    for start in FSTARTS:
        cols = slice(start, start + FB)
        down = turned[:, cols]
        if start % FB:
            down = jnp.concatenate([jnp.zeros((48, 128), bf16), down[:, 128:]], axis=1)
        blocks.append(jnp.concatenate([rows[0, :, cols], rows[1, :, cols], down], axis=1))
    return jnp.stack(blocks)


def x_terms(pieces_of, x):
    got = [pieces_of(x)]
    for d in (2, 1, 3):
        got.append(xshift(pieces_of((x + d) % 4).astype(bf16), d))
    return got


def z_terms(own, other, zh, zl):
    z = 2 * zh + zl
    got = [pick(own, zh)]
    got.append(zshift(pick(own, 1 - zh).astype(bf16), 2))
    for d in (1, 3):
        got.append(zshift(pick(other, ((z + d) % 4) // 2).astype(bf16), d))
    return got


def zh_terms(v, axis, zh):
    mine = lax.dynamic_index_in_dim(v, zh, axis, keepdims=False)
    theirs = lax.dynamic_index_in_dim(v, 1 - zh, axis, keepdims=False).astype(bf16)
    return [mine, lax.ppermute(theirs, "zh", [(0, 1), (1, 0)])]


def total_of(terms):
    total = terms[0].astype(f32)
    for term in terms[1:]:
        total = total + term.astype(f32)
    return total


def to_columns(blocks, y):
    got = jnp.stack(yexchange(lambda j: blocks[j].astype(bf16)))
    return [pick(got, (b - y) % 4) for b in range(4)]


def gather_zh(part, zh):
    other = lax.ppermute(part, "zh", [(0, 1), (1, 0)])
    return jnp.where(zh == 0, jnp.stack([part, other]), jnp.stack([other, part]))


def split_k(v, k, axis):
    mine = lax.dynamic_index_in_dim(v, k, axis, keepdims=False)
    theirs = lax.dynamic_index_in_dim(v, 1 - k, axis, keepdims=False)
    return mine.astype(f32) + kswap(theirs.astype(bf16)).astype(f32)


TILES = ((0, 256), (256, 256), (512, 256), (768, 128))
CHEAP = pl.CostEstimate(flops=1_000_000, bytes_accessed=1_000_000, transcendentals=0)
WIDE = pltpu.CompilerParams(
    dimension_semantics=("arbitrary",), vmem_limit_bytes=50 * 1024 * 1024
)


def load_mixer(source, rows, sems):
    copies = []
    for r in range(2):
        for b in range(4):
            for e in range(8):
                first = 384 * b + 48 * e
                copies.append(
                    pltpu.make_async_copy(
                        source.at[e, r, b],
                        rows.at[r, pl.ds(first, 48)],
                        sems.at[32 * r + 8 * b + e],
                    )
                )
    for copy in copies:
        copy.start()
    for copy in copies:
        copy.wait()


def mixer_kernel(
    half_ref, x0, x1, x2, x3, swap_ref, taps_ref, w_hbm, n_ref, inv_ref, proj0, proj1,
    conv0, conv1, before0, before1, act0, act1, wo0, wo1, p0, p1, p2, p3, w_ref, sems,
):
    load_mixer(w_hbm, w_ref, sems)
    xs = (x0, x1, x2, x3)
    gain = jnp.concatenate([ref[512:528, :] for ref in xs], axis=1)[:1].astype(f32)
    for i in range(4):
        rows = pl.ds(128 * i, 128)
        wide = jnp.concatenate([ref[rows, :] for ref in xs], axis=1).astype(f32)
        inv = lax.rsqrt(jnp.sum(wide * wide, axis=1, keepdims=True) / D + EPSILON)
        inv_ref[rows, :] = inv
        n_ref[rows, :] = (wide * inv * gain).astype(bf16)
    tail = swap_ref[:16, :].astype(f32)
    tail = jnp.where(half_ref[0] == 1, tail, 0.0)
    inv = lax.rsqrt(jnp.sum(tail * tail, axis=1, keepdims=True) / D + EPSILON)
    n_tail = (tail * inv * gain).astype(bf16)
    own_taps = taps_ref[...].astype(f32)
    other_taps = swap_ref[16:32, :192].astype(f32)
    line = lax.broadcasted_iota(jnp.int32, (512, 192), 0)
    acts = (act0, act1)
    for r, taps in ((0, own_taps), (1, other_taps)):
        proj_ref = (proj0, proj1)[r]
        proj_ref[...] = dot(n_ref[...], w_ref[r, :, :576])
        proj_tail = dot(n_tail, w_ref[r, :, :576])
        before = proj_tail[8:, :192] * proj_tail[8:, 384:]
        (before0, before1)[r][...] = before
        mixed = proj_ref[:, :192] * proj_ref[:, 384:576]
        one = jnp.where(line == 0, before[7:8], pltpu.roll(mixed, 1, 0))
        two = jnp.where(
            line == 0, before[6:7], jnp.where(line == 1, before[7:8], pltpu.roll(mixed, 2, 0))
        )
        conv = taps[0:1] * mixed + taps[1:2] * one + taps[2:3] * two
        (conv0, conv1)[r][...] = conv
        acts[r][...] = (proj_ref[:, 192:384] * conv).astype(bf16)
        (wo0, wo1)[r][...] = w_ref[r, :, 640:]
    for j, ref in enumerate((p0, p1, p2, p3)):
        rows = pl.ds(384 * j, 384)
        part = dot_t(act0[...], wo0[rows, :]) + dot_t(act1[...], wo1[rows, :])
        ref[...] = part.astype(ref.dtype)


def mixer_call(half, pieces, swapped, taps, weight, *deps):
    whole = pl.BlockSpec(memory_space=pltpu.VMEM)

    def kernel(*refs):
        mixer_kernel(*refs[:8], *refs[8 + len(deps) :])

    def shape(*dims, kind=f32):
        return jax.ShapeDtypeStruct(dims, kind)

    return pl.pallas_call(
        kernel,
        in_specs=[pl.BlockSpec(memory_space=pltpu.SMEM)]
        + [whole] * 6
        + [pl.BlockSpec(memory_space=pl.ANY)] * (1 + len(deps)),
        out_specs=[whole] * 16,
        out_shape=[shape(512, D, kind=bf16), shape(512, 1)]
        + [shape(512, 576)] * 2
        + [shape(512, 192)] * 2
        + [shape(8, 192)] * 2
        + [shape(512, 192, kind=bf16)] * 2
        + [shape(D, 192, kind=bf16)] * 2
        + [shape(512, 384)]
        + [shape(512, 384, kind=bf16)] * 3,
        scratch_shapes=[pltpu.VMEM((2, D, 832), bf16), pltpu.SemaphoreType.DMA((64,))],
        compiler_params=pltpu.CompilerParams(vmem_limit_bytes=50 * 1024 * 1024),
        cost_estimate=CHEAP,
        name="mixer",
    )(half, *pieces, swapped, taps, weight, *deps)


def stream_kernel(*refs):
    q_refs, s_refs, g_refs = refs[:4], refs[4:8], refs[8:12]
    own_ref, gain_ref, wo0, wo1, proj0, proj1 = refs[12:18]
    sb_ref, grad0, grad1, halo_ref, sg_ref, gain_out = refs[-6:]
    gain = gain_ref[...]
    sums = jnp.zeros((1, 384), f32)
    for i in range(4):
        rows = pl.ds(128 * i, 128)
        stream = jnp.concatenate([ref[rows, :] for ref in s_refs], axis=1).astype(f32)
        inv = lax.rsqrt(jnp.sum(stream * stream, axis=1, keepdims=True) / D + EPSILON)
        hat = stream * inv
        weighted = gain * jnp.concatenate([ref[rows, :] for ref in q_refs], axis=1).astype(f32)
        mean = jnp.sum(weighted * hat, axis=1, keepdims=True) / D
        grads = jnp.concatenate([ref[rows, :] for ref in g_refs], axis=1).astype(f32)
        sb_ref[rows, :] = (grads + inv * (weighted - hat * mean)).astype(bf16)
        own = own_ref[rows, :]
        own_hat = hat[:, :384]
        sg_ref[rows, :] = grads[:, :384] + inv * (gain[:, :384] * own - own_hat * mean)
        sums = sums + jnp.sum(own * own_hat, axis=0, keepdims=True)
    gain_out[...] = sums
    for r in range(2):
        grad_ref = (grad0, grad1)[r]
        grad_ref[...] = dot(sb_ref[...], (wo0, wo1)[r][...])
        halo_ref[1 - r] = grad_ref[:8, :] * (proj0, proj1)[r][:8, 192:384]


def stream_call(two_all, streams, grads, two_grad, gain, w_out, proj, *deps):
    whole = pl.BlockSpec(memory_space=pltpu.VMEM)
    return pl.pallas_call(
        stream_kernel,
        in_specs=[whole] * 18 + [pl.BlockSpec(memory_space=pl.ANY)] * len(deps),
        out_specs=[whole] * 6,
        out_shape=[
            jax.ShapeDtypeStruct((512, D), bf16),
            jax.ShapeDtypeStruct((512, 192), f32),
            jax.ShapeDtypeStruct((512, 192), f32),
            jax.ShapeDtypeStruct((2, 8, 192), f32),
            jax.ShapeDtypeStruct((512, 384), f32),
            jax.ShapeDtypeStruct((1, 384), f32),
        ],
        compiler_params=pltpu.CompilerParams(vmem_limit_bytes=50 * 1024 * 1024),
        cost_estimate=CHEAP,
        name="stream",
    )(*two_all, *streams, *grads, two_grad, gain, *w_out, *proj, *deps)


def back_kernel(
    x0, x1, x2, x3, grad0, grad1, proj0, proj1, conv0, conv1, before0, before1, halo_ref,
    swap_ref, taps_ref, w_hbm, pb0, pb1, p0, p1, p2, p3, gain_out, taps0, taps1, w_ref, sems,
):
    load_mixer(w_hbm, w_ref, sems)
    xs = (x0, x1, x2, x3)
    own_taps = taps_ref[...].astype(f32)
    other_taps = swap_ref[16:32, :192].astype(f32)
    line = lax.broadcasted_iota(jnp.int32, (512, 192), 0)
    for r, taps in ((0, own_taps), (1, other_taps)):
        grad_ref, proj_ref = (grad0, grad1)[r], (proj0, proj1)[r]
        before, halo = (before0, before1)[r][...], halo_ref[r]
        grad = grad_ref[...]
        b_part = proj_ref[:, :192]
        x_part = proj_ref[:, 384:576]
        conv_back = grad * proj_ref[:, 192:384]
        one = jnp.where(line == 511, halo[0:1], pltpu.roll(conv_back, 511, 0))
        two = jnp.where(
            line == 510,
            halo[0:1],
            jnp.where(line == 511, halo[1:2], pltpu.roll(conv_back, 510, 0)),
        )
        mixed_grad = taps[0:1] * conv_back + taps[1:2] * one + taps[2:3] * two
        (pb0, pb1)[r][...] = jnp.concatenate(
            [
                mixed_grad * x_part,
                grad * (conv0, conv1)[r][...],
                mixed_grad * b_part,
                jnp.zeros((512, 64), f32),
            ],
            axis=1,
        ).astype(bf16)
        mixed = b_part * x_part
        lag_one = jnp.where(line == 0, before[7:8], pltpu.roll(mixed, 1, 0))
        lag_two = jnp.where(
            line == 0, before[6:7], jnp.where(line == 1, before[7:8], pltpu.roll(mixed, 2, 0))
        )
        (taps0, taps1)[r][...] = jnp.concatenate(
            [
                jnp.sum(conv_back * lagged, axis=0, keepdims=True)
                for lagged in (mixed, lag_one, lag_two)
            ],
            axis=0,
        )
    gain = jnp.concatenate([ref[512:528, :] for ref in xs], axis=1)[:1].astype(f32)
    ones = jnp.ones((8, D), bf16)
    inner = []
    sums = jnp.zeros((1, D), f32)
    for i in range(4):
        rows = pl.ds(128 * i, 128)
        part = dot_t(pb0[rows, :576], w_ref[0, :, :576]) + dot_t(
            pb1[rows, :576], w_ref[1, :, :576]
        )
        for j, ref in enumerate((p0, p1, p2, p3)):
            ref[rows, :] = part[:, 384 * j : 384 * j + 384].astype(ref.dtype)
        wide = jnp.concatenate([ref[rows, :] for ref in xs], axis=1).astype(f32)
        inv = lax.rsqrt(jnp.sum(wide * wide, axis=1, keepdims=True) / D + EPSILON)
        product = part * (wide * inv)
        sums = sums + jnp.sum(product, axis=0, keepdims=True)
        product = product * gain
        high = product.astype(bf16)
        low = (product - high.astype(f32)).astype(bf16)
        inner.append(dot_t(ones, high) + dot_t(ones, low))
    gain_out[...] = sums
    empty = jnp.zeros((1, 256), f32)
    rows = []
    total = jnp.concatenate(inner, axis=1)[:1]
    high = total.astype(bf16).astype(f32)
    for term in (high, total - high):
        rows.append(term[:, :384])
        rows.append(jnp.concatenate([term[:, 384:], empty], axis=1))
    inner_rows = jnp.concatenate(rows + [jnp.zeros((12, 384), f32)], axis=0)
    for ref in (p0, p1, p2, p3):
        ref[512:528, :] = inner_rows.astype(ref.dtype)


def back_call(pieces, grads, proj, conv, before, halo, swapped, taps, weight, *deps):
    whole = pl.BlockSpec(memory_space=pltpu.VMEM)

    def kernel(*refs):
        back_kernel(*refs[:16], *refs[16 + len(deps) :])

    return pl.pallas_call(
        kernel,
        in_specs=[whole] * 15 + [pl.BlockSpec(memory_space=pl.ANY)] * (1 + len(deps)),
        out_specs=[whole] * 9,
        out_shape=[jax.ShapeDtypeStruct((512, 640), bf16)] * 2
        + [jax.ShapeDtypeStruct((528, 384), f32)]
        + [jax.ShapeDtypeStruct((528, 384), bf16)] * 3
        + [jax.ShapeDtypeStruct((1, D), f32)]
        + [jax.ShapeDtypeStruct((3, 192), f32)] * 2,
        scratch_shapes=[pltpu.VMEM((2, D, 832), bf16), pltpu.SemaphoreType.DMA((64,))],
        compiler_params=pltpu.CompilerParams(vmem_limit_bytes=50 * 1024 * 1024),
        cost_estimate=CHEAP,
        name="back",
    )(*pieces, *grads, *proj, *conv, *before, halo, swapped, taps, weight, *deps)


def ffn_finish(full):
    def kernel(full_ref, gate_ref, down_ref):
        wide = full_ref[...].astype(f32)
        gate_ref[...] = wide[:, :, :48].reshape(2, 384, 384)
        down_ref[...] = wide[:, :, 48:].reshape(384, 384).T

    return pl.pallas_call(
        kernel,
        grid=(9,),
        in_specs=[pl.BlockSpec((8, 2, 72, 384), lambda i: (0, 0, 0, i))],
        out_specs=[
            pl.BlockSpec((2, 384, 384), lambda i: (0, 0, i)),
            pl.BlockSpec((384, 384), lambda i: (i, 0)),
        ],
        out_shape=[
            jax.ShapeDtypeStruct((2, 384, 3456), f32),
            jax.ShapeDtypeStruct((3456, 384), f32),
        ],
        compiler_params=pltpu.CompilerParams(vmem_limit_bytes=50 * 1024 * 1024),
        name="ffn_finish",
    )(full)


def mixer_finish(full, y):
    def kernel(y_ref, full_ref, in_ref, out_ref, own_ref, sum_ref):
        own = jnp.zeros((384, 128), f32)
        total = jnp.zeros((384, 128), f32)
        for b in range(4):
            block = full_ref[:, :, b].astype(f32).reshape(384, FB)
            cols = slice(192 * b, 192 * b + 192)
            for j in range(3):
                in_ref[j, :, cols] = block[:, 192 * j : 192 * j + 192]
            out_ref[cols, :] = block[:, 640:896].T[:192]
            small = block[:, 512:640]
            own = own + jnp.where(y_ref[0] == b, small, 0.0)
            total = total + small
        own_ref[...] = own
        sum_ref[...] = total

    whole = pl.BlockSpec(memory_space=pltpu.VMEM)
    return pl.pallas_call(
        kernel,
        in_specs=[pl.BlockSpec(memory_space=pltpu.SMEM), whole],
        out_specs=[whole] * 4,
        out_shape=[
            jax.ShapeDtypeStruct((3, 384, 768), f32),
            jax.ShapeDtypeStruct((768, 384), f32),
            jax.ShapeDtypeStruct((384, 128), f32),
            jax.ShapeDtypeStruct((384, 128), f32),
        ],
        compiler_params=pltpu.CompilerParams(vmem_limit_bytes=50 * 1024 * 1024),
        name="mixer_finish",
    )(y.astype(jnp.int32)[None], full)


def load_rows(source, rows, sems):
    copies = []
    for b in range(4):
        for e in range(8):
            first = 384 * b + 48 * e
            copies.append(
                pltpu.make_async_copy(
                    source.at[e, b], rows.at[pl.ds(first, 48)], sems.at[8 * b + e]
                )
            )
    for copy in copies:
        copy.start()
    for copy in copies:
        copy.wait()


def ffn_kernel(*refs):
    s_refs, g_refs = refs[:4], refs[4:8]
    gain_ref, w_hbm = refs[8:10]
    n_ref, h_ref, gb_ref, ub_ref = refs[-10:-6]
    p_refs = refs[-6:-2]
    w_ref, sems = refs[-2:]

    @pl.when(pl.program_id(0) == 0)
    def _():
        load_rows(w_hbm, w_ref, sems)

    stream = jnp.concatenate([ref[...] for ref in s_refs], axis=1).astype(f32)
    inv = lax.rsqrt(jnp.sum(stream * stream, axis=1, keepdims=True) / D + EPSILON)
    n_ref[...] = (stream * inv * gain_ref[...]).astype(bf16)
    grads = jnp.concatenate([ref[...] for ref in g_refs], axis=1)
    for first, size in TILES:
        cols = pl.ds(first, size)
        w_pair = jnp.concatenate(
            [w_ref[:, cols], w_ref[:, pl.ds(FB + first, size)]], axis=1
        )
        gate_up = dot(n_ref[...], w_pair)
        gate = gate_up[:, :size]
        up = gate_up[:, size:]
        sig = jax.nn.sigmoid(gate)
        silu = gate * sig
        h_ref[:, cols] = (silu * up).astype(bf16)
        hidden_grad = dot(grads, w_ref[:, pl.ds(2 * FB + first, size)])
        gb_ref[:, cols] = (
            hidden_grad * up * sig * (1.0 + gate * (1.0 - sig))
        ).astype(bf16)
        ub_ref[:, cols] = (hidden_grad * silu).astype(bf16)
    back = jnp.concatenate([gb_ref[...], ub_ref[...]], axis=1)
    parts = jnp.concatenate(
        [dot_t(back, w_ref[pl.ds(512 * i, 512), : 2 * FB]) for i in range(3)], axis=1
    )
    for j in range(4):
        p_refs[j][...] = parts[:, 384 * j : 384 * j + 384].astype(p_refs[j].dtype)


def ffn_call(streams, grads, gain, weight, *deps):
    narrow = pl.BlockSpec((256, 384), lambda i: (i, 0))
    middle = pl.BlockSpec((256, FB), lambda i: (i, 0))
    wide = pl.BlockSpec((256, D), lambda i: (i, 0))
    whole = pl.BlockSpec(memory_space=pl.ANY)
    return pl.pallas_call(
        ffn_kernel,
        grid=(2,),
        in_specs=[narrow] * 8
        + [pl.BlockSpec((1, D), lambda i: (0, 0)), whole]
        + [whole] * len(deps),
        out_specs=[wide] + [middle] * 3 + [narrow] * 4,
        out_shape=[jax.ShapeDtypeStruct((512, D), bf16)]
        + [jax.ShapeDtypeStruct((512, FB), bf16)] * 3
        + [jax.ShapeDtypeStruct((512, 384), f32)]
        + [jax.ShapeDtypeStruct((512, 384), bf16)] * 3,
        scratch_shapes=[pltpu.VMEM((D, 3 * FB), bf16), pltpu.SemaphoreType.DMA((32,))],
        compiler_params=WIDE,
        cost_estimate=pl.CostEstimate(
            flops=8_400_000_000, bytes_accessed=16_000_000, transcendentals=500_000
        ),
        name="ffn",
    )(*streams, *grads, gain, weight, *deps)


def block_kernel(h0_ref, h1_ref, w_ref, out_ref):
    hidden = jnp.where(pl.program_id(1) < 1, h0_ref[...], h1_ref[...])
    out_ref[0, 0] = dot_t(hidden, w_ref[...].reshape(384, FB)).astype(bf16)


def block_call(own, other, weight):
    def where(j, t):
        return (j, t, 0, 0)

    return pl.pallas_call(
        block_kernel,
        grid=(4, 2),
        in_specs=[
            pl.BlockSpec((512, FB), lambda j, t: (0, 0)),
            pl.BlockSpec((512, FB), lambda j, t: (0, 0)),
            pl.BlockSpec((8, None, 48, FB), lambda j, t: (0, j, 0, 2)),
        ],
        out_specs=pl.BlockSpec((1, 1, 512, 384), where),
        out_shape=jax.ShapeDtypeStruct((4, 2, 512, 384), bf16),
        compiler_params=pltpu.CompilerParams(vmem_limit_bytes=50 * 1024 * 1024),
        cost_estimate=pl.CostEstimate(
            flops=2_800_000_000, bytes_accessed=10_000_000, transcendentals=0
        ),
        name="block",
    )(own, other, weight)


def row_sum(v):
    return jnp.sum(v, axis=1, keepdims=True)


def body(
    block_in,
    norm_gain,
    in_weight,
    conv_weight,
    out_weight,
    ffn_gain,
    gate_up_weight,
    down_weight,
    out_grad,
):
    zh = lax.axis_index("zh")
    x = lax.axis_index("x")
    k = lax.axis_index("k")
    zl = lax.axis_index("zl")
    y = lax.axis_index("y")

    first = (2 * x + k) * 48
    mixer_own = to_owners(pack_mixer(in_weight, out_weight, first), y)
    sent = jnp.concatenate(
        [block_in, norm_gain[None], ffn_gain[None], jnp.zeros((14, 384), bf16)], axis=0
    )
    sent = ygather(sent)
    gain_one = jnp.concatenate([v[512:513] for v in sent], axis=1).astype(f32)
    gain_two = jnp.concatenate([v[513:514] for v in sent], axis=1).astype(f32)

    swapped = jnp.concatenate(
        [
            jnp.concatenate([v[496:512] for v in sent], axis=1),
            jnp.pad(conv_weight, ((0, 13), (0, D - 192))),
        ],
        axis=0,
    )
    swapped = zswap(swapped)

    mixer_both = jnp.stack([mixer_own, zexchange(mixer_own)])
    w_mixer = lax.all_gather(mixer_both, ("x", "k"))

    blocks = pack_ffn(gate_up_weight, down_weight, first)
    blocks, sent = lax.optimization_barrier((blocks, sent))
    ffn = to_owners(blocks, y)
    ffn, swapped, out_grad_late = lax.optimization_barrier((ffn, swapped, out_grad))
    w_ffn = lax.all_gather(ffn, ("x", "k"))
    grad_pieces = ygather(out_grad_late)
    half = zl.astype(jnp.int32)[None]
    results = mixer_call(half, sent, swapped, conv_weight, w_mixer)
    normed_one, inv_one = results[:2]
    proj, conv, before, acts, w_out = (results[i : i + 2] for i in range(2, 12, 2))

    out_parts, grad_pieces = lax.optimization_barrier((results[12:], grad_pieces))
    stream_own = block_in.astype(f32) + yreduce(out_parts)
    grads_own = jnp.concatenate(grad_pieces, axis=1)
    grads_other = zswap(grads_own)
    stream_sent = stream_own.astype(bf16)
    other = zswap(stream_sent)
    pieces_own = ygather(stream_sent)
    pieces_other = ygather(other)
    other_grads = [grads_other[:, 384 * j : 384 * j + 384] for j in range(4)]
    half_own = ffn_call(pieces_own, grad_pieces, gain_two, w_ffn)
    half_other = ffn_call(pieces_other, other_grads, gain_two, w_ffn, half_own[0])
    own_terms = yexchange(lambda j: half_own[4 + j])
    own_terms, half_other = lax.optimization_barrier((own_terms, half_other))
    other_terms = yexchange(lambda j: half_other[4 + j])
    normed_two = jnp.concatenate([half_own[0], half_other[0]], axis=0)
    theirs = t_dot(
        normed_two,
        jnp.concatenate(
            [jnp.where(k == 0, half[3], half[2]) for half in (half_own, half_other)], axis=0
        ),
    ).astype(bf16)
    hidden = jnp.concatenate([half_own[1], half_other[1]], axis=0)
    grads_all = jnp.concatenate([grads_own, grads_other], axis=0)
    down_grad = t_dot(grads_all, hidden)
    block_parts = block_call(half_own[1], half_other[1], w_ffn)
    other_terms, half_own, half_other, theirs, down_grad, block_parts = (
        lax.optimization_barrier(
            (other_terms, half_own, half_other, theirs, down_grad, block_parts)
        )
    )
    theirs = kswap(theirs)
    sum_other = total_of(other_terms)
    sum_own = total_of(own_terms)
    from_other = zswap(sum_other.astype(bf16))
    two_grad = sum_own + from_other.astype(f32)

    two_all = ygather(two_grad.astype(bf16))

    mine = t_dot(
        normed_two,
        jnp.concatenate(
            [jnp.where(k == 0, half[2], half[3]) for half in (half_own, half_other)], axis=0
        ),
    )
    gate_up_grad = (mine + theirs.astype(f32)).reshape(4, 4, 2, 48, FB)
    down_grad = split_k(down_grad.reshape(4, 2, 192, FB), k, 1).reshape(4, 4, 2, 24, FB)
    ffn = jnp.concatenate([gate_up_grad, down_grad], axis=3).astype(bf16)
    ffn = jnp.stack([pick(ffn, (b - y) % 4) for b in range(4)])
    ffn, two_all = lax.optimization_barrier((ffn, two_all))
    ffn = ffn.transpose(2, 1, 0, 3, 4).reshape(32, 72, FB)
    ffn = lax.all_to_all(ffn, ("zh", "x", "y"), 0, 0, tiled=True)

    stream_back, *grads, halo, own_stream_grad, gain_two_part = stream_call(
        two_all, pieces_own, grad_pieces, two_grad, gain_two, w_out, proj
    )
    halo = lax.ppermute(halo, "zl", [(1, 0)])
    results = back_call(
        sent, grads, proj, conv, before, halo, swapped, conv_weight, w_mixer
    )
    proj_back = results[:2]
    gain_one_part, *conv_parts = results[6:]
    one_parts = results[2:6]
    tails = []
    for r in range(2):
        taps_part = conv_parts[r].reshape(-1)
        rest = jnp.concatenate([taps_part[384:], jnp.zeros((192,), f32)])
        small = jnp.stack([gain_two_part[0], taps_part[:384], rest], axis=1)
        small = jnp.pad(small, ((0, D - 384), (577, 60)))
        small = small + jnp.pad(gain_one_part.T, ((0, 0), (576, 63)))
        padded = jnp.pad(acts[r], ((0, 0), (0, 64)))
        tails.append((t_dot(normed_one, proj_back[r]) + small, t_dot(stream_back, padded)))

    def tail_half(index):
        halves = []
        for pair in tails:
            rows = [
                lax.dynamic_index_in_dim(v.reshape(4, 2, 192, -1), index, 1, keepdims=False)
                for v in pair
            ]
            halves.append(jnp.concatenate(rows, axis=2))
        return jnp.stack(halves)

    theirs = tail_half(1 - k)
    theirs, ffn, one_parts, block_parts = lax.optimization_barrier(
        (theirs, ffn, one_parts, block_parts)
    )
    one_terms = yexchange(lambda j: one_parts[j])
    mixer = tail_half(k) + kswap(theirs.astype(bf16)).astype(f32)
    mixer, one_terms = lax.optimization_barrier((mixer, one_terms))
    cols = list(jnp.sum(ffn.reshape(8, 4, 72, FB).astype(f32), axis=0).astype(bf16))
    part = jnp.concatenate(cols[:3] + [cols[3][:, 128:]], axis=1)
    part = gather_zh(part, zh)
    mixer = jnp.stack([pick(mixer.swapaxes(0, 1), (b - y) % 4) for b in range(4)])
    mixer = jnp.where(zl == 0, mixer, mixer[:, ::-1]).astype(bf16)
    mixer, part = lax.optimization_barrier((mixer, part))
    full = lax.all_gather(part, ("k", "x"))
    gate_up_out, down_out = ffn_finish(full)
    mixer = mixer.reshape(4, 2, 4, 2, 24, FB).transpose(3, 2, 1, 0, 4, 5)
    mixer = lax.all_to_all(
        mixer.reshape(64, 24, FB), ("zh", "x", "zl", "y"), 0, 0, tiled=True
    )
    block_terms = yexchange(lambda j: block_parts[j])
    one_sum = total_of(one_terms)
    one_grad = one_sum[:512]
    inner_one = one_sum[512:514].reshape(-1)[:512] + one_sum[514:516].reshape(-1)[:512]
    own_hat = block_in.astype(f32) * inv_one
    in_grad = own_stream_grad + inv_one * (
        gain_one[:, :384] * one_grad - own_hat * (inner_one / D)[:, None]
    )
    in_grad = in_grad.astype(bf16)
    cols = jnp.sum(mixer.reshape(16, 4, 24, FB).astype(f32), axis=0).astype(bf16)
    part = gather_zh(cols, zh)
    part, block_terms = lax.optimization_barrier((part, block_terms))
    block_sum = total_of(block_terms)
    block_out = stream_own + block_sum[0] + zswap(block_sum[1].astype(bf16)).astype(f32)
    block_out = block_out.astype(bf16)
    full = lax.all_gather(part, ("k", "x"))
    full, gate_up_out, down_out, in_grad, block_out = lax.optimization_barrier(
        (full, gate_up_out, down_out, in_grad, block_out)
    )
    in_out, out_out, own_small, sum_small = mixer_finish(full, y)
    gain_one_out = sum_small[:, 64]
    gain_two_out = own_small[:, 65]
    conv_out = jnp.concatenate([own_small[:, 66], own_small[:192, 67]]).reshape(3, 192)
    return (
        block_out,
        in_grad,
        gain_one_out,
        in_out,
        conv_out,
        out_out,
        gain_two_out,
        gate_up_out,
        down_out,
    )


def solution(mesh):
    devices = mesh.devices.reshape(2, 4, 2, 2, 4)
    grid = Mesh(devices, ("zh", "x", "k", "zl", "y"))
    tokens = P(("zh", "x", "k", "zl"), "y")
    first = P(None, "y", "zl")
    second = P("zl", "y")
    in_specs = (
        tokens,
        P("y"),
        first,
        P(None, ("zl", "y")),
        second,
        P("y"),
        first,
        second,
        tokens,
    )
    out_specs = (
        tokens,
        tokens,
        P("y"),
        first,
        P(None, ("zl", "y")),
        second,
        P("y"),
        first,
        second,
    )
    return jax.shard_map(body, mesh=grid, in_specs=in_specs, out_specs=out_specs, check_vma=False)
```

```python
import functools

import jax
import jax.numpy as jnp
from jax import lax
from jax.experimental import pallas as pl
from jax.experimental.pallas import tpu as pltpu
from jax.sharding import Mesh, PartitionSpec as P

D = 1536
LEN = 1024
EPSILON = 1e-05
FB = 896
FSTARTS = (0, 896, 1792, 2560)

bf16 = jnp.bfloat16
f32 = jnp.float32


def yshift(v, d):
    return lax.ppermute(v, "y", [(i, (i + d) % 4) for i in range(4)])


def xshift(v, d):
    return lax.ppermute(v, "x", [(i, (i + d) % 4) for i in range(4)])


def zshift(v, d):
    return lax.ppermute(v, ("zh", "zl"), [(i, (i + d) % 4) for i in range(4)])


def zswap(v):
    return lax.ppermute(v, "zl", [(0, 1), (1, 0)])


def kswap(v):
    return lax.ppermute(v, "k", [(0, 1), (1, 0)])


def ygather(v):
    two = yshift(v, 2)
    return [v, yshift(v, 3), two, yshift(v, 1)]


def yexchange(block_for):
    two = yshift(block_for(2), 2)
    one = yshift(block_for(1), 1)
    three = yshift(block_for(3), 3)
    return [block_for(0), three, two, one]


def yreduce(pieces):
    got = yexchange(lambda j: pieces[j].astype(bf16) if j else pieces[0])
    return got[0].astype(f32) + got[1].astype(f32) + got[2].astype(f32) + got[3].astype(f32)


def zexchange(v):
    half = v.shape[0] // 2
    up = zshift(v[:half], 1)
    down = zshift(v[half:], 3)
    return jnp.concatenate([up, down], axis=0)


def pick(stacked, index):
    return lax.dynamic_index_in_dim(stacked, index, 0, keepdims=False)


def dot(a, b):
    return jnp.dot(a, b, preferred_element_type=f32)


def dot_t(a, b):
    return lax.dot_general(a, b, (((1,), (1,)), ((), ())), preferred_element_type=f32)


def t_dot(a, b):
    return lax.dot_general(a, b, (((0,), (0,)), ((), ())), preferred_element_type=f32)


def after(v, *deps):
    for dep in deps:
        last = lax.slice(dep, [n - 1 for n in dep.shape], dep.shape).reshape(())
        v = v + (last * 0).astype(v.dtype)
    return v


def both(k, mine, other, axis):
    return jnp.where(
        k == 0,
        jnp.concatenate([mine, other], axis=axis),
        jnp.concatenate([other, mine], axis=axis),
    )


def to_owners(blocks, y):
    return jnp.stack(yexchange(lambda j: pick(blocks, (y + j) % 4)))


def pack_mixer(in_weight, out_weight, first):
    rows = lax.dynamic_slice_in_dim(in_weight, first, 48, axis=1)
    turned = lax.dynamic_slice_in_dim(out_weight.T, first, 48, axis=0)
    blocks = []
    for b in range(4):
        cols = slice(192 * b, 192 * b + 192)
        blocks.append(
            jnp.concatenate(
                [
                    rows[0, :, cols],
                    rows[1, :, cols],
                    rows[2, :, cols],
                    jnp.zeros((48, 64), bf16),
                    turned[:, cols],
                ],
                axis=1,
            )
        )
    return jnp.stack(blocks)


def pack_ffn(gate_up_weight, down_weight, first):
    rows = lax.dynamic_slice_in_dim(gate_up_weight, first, 48, axis=1)
    turned = lax.dynamic_slice_in_dim(down_weight.T, first, 48, axis=0)
    blocks = []
    for start in FSTARTS:
        cols = slice(start, start + FB)
        down = turned[:, cols]
        if start % FB:
            down = jnp.concatenate([jnp.zeros((48, 128), bf16), down[:, 128:]], axis=1)
        blocks.append(jnp.concatenate([rows[0, :, cols], rows[1, :, cols], down], axis=1))
    return jnp.stack(blocks)


def x_terms(pieces_of, x):
    got = [pieces_of(x)]
    for d in (2, 1, 3):
        got.append(xshift(pieces_of((x + d) % 4).astype(bf16), d))
    return got


def z_terms(own, other, zh, zl):
    z = 2 * zh + zl
    got = [pick(own, zh)]
    got.append(zshift(pick(own, 1 - zh).astype(bf16), 2))
    for d in (1, 3):
        got.append(zshift(pick(other, ((z + d) % 4) // 2).astype(bf16), d))
    return got


def zh_terms(v, axis, zh):
    mine = lax.dynamic_index_in_dim(v, zh, axis, keepdims=False)
    theirs = lax.dynamic_index_in_dim(v, 1 - zh, axis, keepdims=False).astype(bf16)
    return [mine, lax.ppermute(theirs, "zh", [(0, 1), (1, 0)])]


def total_of(terms):
    total = terms[0].astype(f32)
    for term in terms[1:]:
        total = total + term.astype(f32)
    return total


def to_columns(blocks, y):
    got = jnp.stack(yexchange(lambda j: blocks[j].astype(bf16)))
    return [pick(got, (b - y) % 4) for b in range(4)]


def gather_zh(part, zh):
    other = lax.ppermute(part, "zh", [(0, 1), (1, 0)])
    return jnp.where(zh == 0, jnp.stack([part, other]), jnp.stack([other, part]))


def split_k(v, k, axis):
    mine = lax.dynamic_index_in_dim(v, k, axis, keepdims=False)
    theirs = lax.dynamic_index_in_dim(v, 1 - k, axis, keepdims=False)
    return mine.astype(f32) + kswap(theirs.astype(bf16)).astype(f32)


TILES = ((0, 256), (256, 256), (512, 256), (768, 128))
CHEAP = pl.CostEstimate(flops=1_000_000, bytes_accessed=1_000_000, transcendentals=0)
WIDE = pltpu.CompilerParams(
    dimension_semantics=("arbitrary",), vmem_limit_bytes=50 * 1024 * 1024
)


def load_mixer(source, rows, sems):
    copies = []
    for r in range(2):
        for b in range(4):
            for e in range(8):
                first = 384 * b + 48 * e
                copies.append(
                    pltpu.make_async_copy(
                        source.at[e, r, b],
                        rows.at[r, pl.ds(first, 48)],
                        sems.at[32 * r + 8 * b + e],
                    )
                )
    for copy in copies:
        copy.start()
    for copy in copies:
        copy.wait()


def mixer_kernel(
    half_ref, x0, x1, x2, x3, swap_ref, taps_ref, w_hbm, n_ref, inv_ref, proj0, proj1,
    conv0, conv1, before0, before1, act0, act1, wo0, wo1, p0, p1, p2, p3, w_ref, sems,
):
    load_mixer(w_hbm, w_ref, sems)
    xs = (x0, x1, x2, x3)
    gain = jnp.concatenate([ref[512:528, :] for ref in xs], axis=1)[:1].astype(f32)
    for i in range(4):
        rows = pl.ds(128 * i, 128)
        wide = jnp.concatenate([ref[rows, :] for ref in xs], axis=1).astype(f32)
        inv = lax.rsqrt(jnp.sum(wide * wide, axis=1, keepdims=True) / D + EPSILON)
        inv_ref[rows, :] = inv
        n_ref[rows, :] = (wide * inv * gain).astype(bf16)
    tail = swap_ref[:16, :].astype(f32)
    tail = jnp.where(half_ref[0] == 1, tail, 0.0)
    inv = lax.rsqrt(jnp.sum(tail * tail, axis=1, keepdims=True) / D + EPSILON)
    n_tail = (tail * inv * gain).astype(bf16)
    own_taps = taps_ref[...].astype(f32)
    other_taps = swap_ref[16:32, :192].astype(f32)
    line = lax.broadcasted_iota(jnp.int32, (512, 192), 0)
    acts = (act0, act1)
    for r, taps in ((0, own_taps), (1, other_taps)):
        proj_ref = (proj0, proj1)[r]
        proj_ref[...] = dot(n_ref[...], w_ref[r, :, :576])
        proj_tail = dot(n_tail, w_ref[r, :, :576])
        before = proj_tail[8:, :192] * proj_tail[8:, 384:]
        (before0, before1)[r][...] = before
        mixed = proj_ref[:, :192] * proj_ref[:, 384:576]
        one = jnp.where(line == 0, before[7:8], pltpu.roll(mixed, 1, 0))
        two = jnp.where(
            line == 0, before[6:7], jnp.where(line == 1, before[7:8], pltpu.roll(mixed, 2, 0))
        )
        conv = taps[0:1] * mixed + taps[1:2] * one + taps[2:3] * two
        (conv0, conv1)[r][...] = conv
        acts[r][...] = (proj_ref[:, 192:384] * conv).astype(bf16)
        (wo0, wo1)[r][...] = w_ref[r, :, 640:]
    for j, ref in enumerate((p0, p1, p2, p3)):
        rows = pl.ds(384 * j, 384)
        part = dot_t(act0[...], wo0[rows, :]) + dot_t(act1[...], wo1[rows, :])
        ref[...] = part.astype(ref.dtype)


def mixer_call(half, pieces, swapped, taps, weight, *deps):
    whole = pl.BlockSpec(memory_space=pltpu.VMEM)

    def kernel(*refs):
        mixer_kernel(*refs[:8], *refs[8 + len(deps) :])

    def shape(*dims, kind=f32):
        return jax.ShapeDtypeStruct(dims, kind)

    return pl.pallas_call(
        kernel,
        in_specs=[pl.BlockSpec(memory_space=pltpu.SMEM)]
        + [whole] * 6
        + [pl.BlockSpec(memory_space=pl.ANY)] * (1 + len(deps)),
        out_specs=[whole] * 16,
        out_shape=[shape(512, D, kind=bf16), shape(512, 1)]
        + [shape(512, 576)] * 2
        + [shape(512, 192)] * 2
        + [shape(8, 192)] * 2
        + [shape(512, 192, kind=bf16)] * 2
        + [shape(D, 192, kind=bf16)] * 2
        + [shape(512, 384)]
        + [shape(512, 384, kind=bf16)] * 3,
        scratch_shapes=[pltpu.VMEM((2, D, 832), bf16), pltpu.SemaphoreType.DMA((64,))],
        compiler_params=pltpu.CompilerParams(vmem_limit_bytes=50 * 1024 * 1024),
        cost_estimate=CHEAP,
        name="mixer",
    )(half, *pieces, swapped, taps, weight, *deps)


def stream_kernel(*refs):
    q_refs, s_refs, g_refs = refs[:4], refs[4:8], refs[8:12]
    own_ref, gain_ref, wo0, wo1, proj0, proj1 = refs[12:18]
    sb_ref, grad0, grad1, halo_ref, sg_ref, gain_out = refs[-6:]
    gain = gain_ref[...]
    sums = jnp.zeros((1, 384), f32)
    for i in range(4):
        rows = pl.ds(128 * i, 128)
        stream = jnp.concatenate([ref[rows, :] for ref in s_refs], axis=1).astype(f32)
        inv = lax.rsqrt(jnp.sum(stream * stream, axis=1, keepdims=True) / D + EPSILON)
        hat = stream * inv
        weighted = gain * jnp.concatenate([ref[rows, :] for ref in q_refs], axis=1).astype(f32)
        mean = jnp.sum(weighted * hat, axis=1, keepdims=True) / D
        grads = jnp.concatenate([ref[rows, :] for ref in g_refs], axis=1).astype(f32)
        sb_ref[rows, :] = (grads + inv * (weighted - hat * mean)).astype(bf16)
        own = own_ref[rows, :]
        own_hat = hat[:, :384]
        sg_ref[rows, :] = grads[:, :384] + inv * (gain[:, :384] * own - own_hat * mean)
        sums = sums + jnp.sum(own * own_hat, axis=0, keepdims=True)
    gain_out[...] = sums
    for r in range(2):
        grad_ref = (grad0, grad1)[r]
        grad_ref[...] = dot(sb_ref[...], (wo0, wo1)[r][...])
        halo_ref[1 - r] = grad_ref[:8, :] * (proj0, proj1)[r][:8, 192:384]


def stream_call(two_all, streams, grads, two_grad, gain, w_out, proj, *deps):
    whole = pl.BlockSpec(memory_space=pltpu.VMEM)
    return pl.pallas_call(
        stream_kernel,
        in_specs=[whole] * 18 + [pl.BlockSpec(memory_space=pl.ANY)] * len(deps),
        out_specs=[whole] * 6,
        out_shape=[
            jax.ShapeDtypeStruct((512, D), bf16),
            jax.ShapeDtypeStruct((512, 192), f32),
            jax.ShapeDtypeStruct((512, 192), f32),
            jax.ShapeDtypeStruct((2, 8, 192), f32),
            jax.ShapeDtypeStruct((512, 384), f32),
            jax.ShapeDtypeStruct((1, 384), f32),
        ],
        compiler_params=pltpu.CompilerParams(vmem_limit_bytes=50 * 1024 * 1024),
        cost_estimate=CHEAP,
        name="stream",
    )(*two_all, *streams, *grads, two_grad, gain, *w_out, *proj, *deps)


def back_kernel(
    x0, x1, x2, x3, grad0, grad1, proj0, proj1, conv0, conv1, before0, before1, halo_ref,
    swap_ref, taps_ref, w_hbm, pb0, pb1, p0, p1, p2, p3, gain_out, taps0, taps1, w_ref, sems,
):
    load_mixer(w_hbm, w_ref, sems)
    xs = (x0, x1, x2, x3)
    own_taps = taps_ref[...].astype(f32)
    other_taps = swap_ref[16:32, :192].astype(f32)
    line = lax.broadcasted_iota(jnp.int32, (512, 192), 0)
    for r, taps in ((0, own_taps), (1, other_taps)):
        grad_ref, proj_ref = (grad0, grad1)[r], (proj0, proj1)[r]
        before, halo = (before0, before1)[r][...], halo_ref[r]
        grad = grad_ref[...]
        b_part = proj_ref[:, :192]
        x_part = proj_ref[:, 384:576]
        conv_back = grad * proj_ref[:, 192:384]
        one = jnp.where(line == 511, halo[0:1], pltpu.roll(conv_back, 511, 0))
        two = jnp.where(
            line == 510,
            halo[0:1],
            jnp.where(line == 511, halo[1:2], pltpu.roll(conv_back, 510, 0)),
        )
        mixed_grad = taps[0:1] * conv_back + taps[1:2] * one + taps[2:3] * two
        (pb0, pb1)[r][...] = jnp.concatenate(
            [
                mixed_grad * x_part,
                grad * (conv0, conv1)[r][...],
                mixed_grad * b_part,
                jnp.zeros((512, 64), f32),
            ],
            axis=1,
        ).astype(bf16)
        mixed = b_part * x_part
        lag_one = jnp.where(line == 0, before[7:8], pltpu.roll(mixed, 1, 0))
        lag_two = jnp.where(
            line == 0, before[6:7], jnp.where(line == 1, before[7:8], pltpu.roll(mixed, 2, 0))
        )
        (taps0, taps1)[r][...] = jnp.concatenate(
            [
                jnp.sum(conv_back * lagged, axis=0, keepdims=True)
                for lagged in (mixed, lag_one, lag_two)
            ],
            axis=0,
        )
    gain = jnp.concatenate([ref[512:528, :] for ref in xs], axis=1)[:1].astype(f32)
    ones = jnp.ones((8, D), bf16)
    inner = []
    sums = jnp.zeros((1, D), f32)
    for i in range(4):
        rows = pl.ds(128 * i, 128)
        part = dot_t(pb0[rows, :576], w_ref[0, :, :576]) + dot_t(
            pb1[rows, :576], w_ref[1, :, :576]
        )
        for j, ref in enumerate((p0, p1, p2, p3)):
            ref[rows, :] = part[:, 384 * j : 384 * j + 384].astype(ref.dtype)
        wide = jnp.concatenate([ref[rows, :] for ref in xs], axis=1).astype(f32)
        inv = lax.rsqrt(jnp.sum(wide * wide, axis=1, keepdims=True) / D + EPSILON)
        product = part * (wide * inv)
        sums = sums + jnp.sum(product, axis=0, keepdims=True)
        product = product * gain
        high = product.astype(bf16)
        low = (product - high.astype(f32)).astype(bf16)
        inner.append(dot_t(ones, high) + dot_t(ones, low))
    gain_out[...] = sums
    empty = jnp.zeros((1, 256), f32)
    rows = []
    total = jnp.concatenate(inner, axis=1)[:1]
    high = total.astype(bf16).astype(f32)
    for term in (high, total - high):
        rows.append(term[:, :384])
        rows.append(jnp.concatenate([term[:, 384:], empty], axis=1))
    inner_rows = jnp.concatenate(rows + [jnp.zeros((12, 384), f32)], axis=0)
    for ref in (p0, p1, p2, p3):
        ref[512:528, :] = inner_rows.astype(ref.dtype)


def back_call(pieces, grads, proj, conv, before, halo, swapped, taps, weight, *deps):
    whole = pl.BlockSpec(memory_space=pltpu.VMEM)

    def kernel(*refs):
        back_kernel(*refs[:16], *refs[16 + len(deps) :])

    return pl.pallas_call(
        kernel,
        in_specs=[whole] * 15 + [pl.BlockSpec(memory_space=pl.ANY)] * (1 + len(deps)),
        out_specs=[whole] * 9,
        out_shape=[jax.ShapeDtypeStruct((512, 640), bf16)] * 2
        + [jax.ShapeDtypeStruct((528, 384), f32)]
        + [jax.ShapeDtypeStruct((528, 384), bf16)] * 3
        + [jax.ShapeDtypeStruct((1, D), f32)]
        + [jax.ShapeDtypeStruct((3, 192), f32)] * 2,
        scratch_shapes=[pltpu.VMEM((2, D, 832), bf16), pltpu.SemaphoreType.DMA((64,))],
        compiler_params=pltpu.CompilerParams(vmem_limit_bytes=50 * 1024 * 1024),
        cost_estimate=CHEAP,
        name="back",
    )(*pieces, *grads, *proj, *conv, *before, halo, swapped, taps, weight, *deps)


def ffn_finish(full):
    def kernel(full_ref, gate_ref, down_ref):
        wide = full_ref[...].astype(f32)
        gate_ref[...] = wide[:, :, :48].reshape(2, 384, 384)
        down_ref[...] = wide[:, :, 48:].reshape(384, 384).T

    return pl.pallas_call(
        kernel,
        grid=(9,),
        in_specs=[pl.BlockSpec((8, 2, 72, 384), lambda i: (0, 0, 0, i))],
        out_specs=[
            pl.BlockSpec((2, 384, 384), lambda i: (0, 0, i)),
            pl.BlockSpec((384, 384), lambda i: (i, 0)),
        ],
        out_shape=[
            jax.ShapeDtypeStruct((2, 384, 3456), f32),
            jax.ShapeDtypeStruct((3456, 384), f32),
        ],
        compiler_params=pltpu.CompilerParams(vmem_limit_bytes=50 * 1024 * 1024),
        name="ffn_finish",
    )(full)


def mixer_finish(full, y):
    def kernel(y_ref, full_ref, in_ref, out_ref, own_ref, sum_ref):
        own = jnp.zeros((384, 128), f32)
        total = jnp.zeros((384, 128), f32)
        for b in range(4):
            block = full_ref[:, :, b].astype(f32).reshape(384, FB)
            cols = slice(192 * b, 192 * b + 192)
            for j in range(3):
                in_ref[j, :, cols] = block[:, 192 * j : 192 * j + 192]
            out_ref[cols, :] = block[:, 640:896].T[:192]
            small = block[:, 512:640]
            own = own + jnp.where(y_ref[0] == b, small, 0.0)
            total = total + small
        own_ref[...] = own
        sum_ref[...] = total

    whole = pl.BlockSpec(memory_space=pltpu.VMEM)
    return pl.pallas_call(
        kernel,
        in_specs=[pl.BlockSpec(memory_space=pltpu.SMEM), whole],
        out_specs=[whole] * 4,
        out_shape=[
            jax.ShapeDtypeStruct((3, 384, 768), f32),
            jax.ShapeDtypeStruct((768, 384), f32),
            jax.ShapeDtypeStruct((384, 128), f32),
            jax.ShapeDtypeStruct((384, 128), f32),
        ],
        compiler_params=pltpu.CompilerParams(vmem_limit_bytes=50 * 1024 * 1024),
        name="mixer_finish",
    )(y.astype(jnp.int32)[None], full)


def load_rows(source, rows, sems):
    copies = []
    for b in range(4):
        for e in range(8):
            first = 384 * b + 48 * e
            copies.append(
                pltpu.make_async_copy(
                    source.at[e, b], rows.at[pl.ds(first, 48)], sems.at[8 * b + e]
                )
            )
    for copy in copies:
        copy.start()
    for copy in copies:
        copy.wait()


def ffn_kernel(*refs):
    s_refs, g_refs = refs[:4], refs[4:8]
    gain_ref, w_hbm = refs[8:10]
    n_ref, h_ref, gb_ref, ub_ref = refs[-10:-6]
    p_refs = refs[-6:-2]
    w_ref, sems = refs[-2:]

    @pl.when(pl.program_id(0) == 0)
    def _():
        load_rows(w_hbm, w_ref, sems)

    stream = jnp.concatenate([ref[...] for ref in s_refs], axis=1).astype(f32)
    inv = lax.rsqrt(jnp.sum(stream * stream, axis=1, keepdims=True) / D + EPSILON)
    n_ref[...] = (stream * inv * gain_ref[...]).astype(bf16)
    grads = jnp.concatenate([ref[...] for ref in g_refs], axis=1)
    for first, size in TILES:
        cols = pl.ds(first, size)
        w_pair = jnp.concatenate(
            [w_ref[:, cols], w_ref[:, pl.ds(FB + first, size)]], axis=1
        )
        gate_up = dot(n_ref[...], w_pair)
        gate = gate_up[:, :size]
        up = gate_up[:, size:]
        sig = jax.nn.sigmoid(gate)
        silu = gate * sig
        h_ref[:, cols] = (silu * up).astype(bf16)
        hidden_grad = dot(grads, w_ref[:, pl.ds(2 * FB + first, size)])
        gb_ref[:, cols] = (
            hidden_grad * up * sig * (1.0 + gate * (1.0 - sig))
        ).astype(bf16)
        ub_ref[:, cols] = (hidden_grad * silu).astype(bf16)
    back = jnp.concatenate([gb_ref[...], ub_ref[...]], axis=1)
    parts = jnp.concatenate(
        [dot_t(back, w_ref[pl.ds(512 * i, 512), : 2 * FB]) for i in range(3)], axis=1
    )
    for j in range(4):
        p_refs[j][...] = parts[:, 384 * j : 384 * j + 384].astype(p_refs[j].dtype)


def ffn_call(streams, grads, gain, weight, *deps):
    narrow = pl.BlockSpec((256, 384), lambda i: (i, 0))
    middle = pl.BlockSpec((256, FB), lambda i: (i, 0))
    wide = pl.BlockSpec((256, D), lambda i: (i, 0))
    whole = pl.BlockSpec(memory_space=pl.ANY)
    return pl.pallas_call(
        ffn_kernel,
        grid=(2,),
        in_specs=[narrow] * 8
        + [pl.BlockSpec((1, D), lambda i: (0, 0)), whole]
        + [whole] * len(deps),
        out_specs=[wide] + [middle] * 3 + [narrow] * 4,
        out_shape=[jax.ShapeDtypeStruct((512, D), bf16)]
        + [jax.ShapeDtypeStruct((512, FB), bf16)] * 3
        + [jax.ShapeDtypeStruct((512, 384), f32)]
        + [jax.ShapeDtypeStruct((512, 384), bf16)] * 3,
        scratch_shapes=[pltpu.VMEM((D, 3 * FB), bf16), pltpu.SemaphoreType.DMA((32,))],
        compiler_params=WIDE,
        cost_estimate=pl.CostEstimate(
            flops=8_400_000_000, bytes_accessed=16_000_000, transcendentals=500_000
        ),
        name="ffn",
    )(*streams, *grads, gain, weight, *deps)


def block_kernel(h0_ref, h1_ref, w_ref, out_ref):
    hidden = jnp.where(pl.program_id(1) < 1, h0_ref[...], h1_ref[...])
    out_ref[0, 0] = dot_t(hidden, w_ref[...].reshape(384, FB)).astype(bf16)


def block_call(own, other, weight):
    def where(j, t):
        return (j, t, 0, 0)

    return pl.pallas_call(
        block_kernel,
        grid=(4, 2),
        in_specs=[
            pl.BlockSpec((512, FB), lambda j, t: (0, 0)),
            pl.BlockSpec((512, FB), lambda j, t: (0, 0)),
            pl.BlockSpec((8, None, 48, FB), lambda j, t: (0, j, 0, 2)),
        ],
        out_specs=pl.BlockSpec((1, 1, 512, 384), where),
        out_shape=jax.ShapeDtypeStruct((4, 2, 512, 384), bf16),
        compiler_params=pltpu.CompilerParams(vmem_limit_bytes=50 * 1024 * 1024),
        cost_estimate=pl.CostEstimate(
            flops=2_800_000_000, bytes_accessed=10_000_000, transcendentals=0
        ),
        name="block",
    )(own, other, weight)


def row_sum(v):
    return jnp.sum(v, axis=1, keepdims=True)


def body(
    block_in,
    norm_gain,
    in_weight,
    conv_weight,
    out_weight,
    ffn_gain,
    gate_up_weight,
    down_weight,
    out_grad,
):
    zh = lax.axis_index("zh")
    x = lax.axis_index("x")
    k = lax.axis_index("k")
    zl = lax.axis_index("zl")
    y = lax.axis_index("y")

    first = (2 * x + k) * 48
    mixer_own = to_owners(pack_mixer(in_weight, out_weight, first), y)
    sent = jnp.concatenate(
        [block_in, norm_gain[None], ffn_gain[None], jnp.zeros((14, 384), bf16)], axis=0
    )
    sent = ygather(sent)
    gain_one = jnp.concatenate([v[512:513] for v in sent], axis=1).astype(f32)
    gain_two = jnp.concatenate([v[513:514] for v in sent], axis=1).astype(f32)

    swapped = jnp.concatenate(
        [
            jnp.concatenate([v[496:512] for v in sent], axis=1),
            jnp.pad(conv_weight, ((0, 13), (0, D - 192))),
        ],
        axis=0,
    )
    swapped = zswap(swapped)

    mixer_both = jnp.stack([mixer_own, zexchange(mixer_own)])
    w_mixer = lax.all_gather(mixer_both, ("x", "k"))

    blocks = pack_ffn(gate_up_weight, down_weight, first)
    blocks, sent = lax.optimization_barrier((blocks, sent))
    ffn = to_owners(blocks, y)
    ffn, swapped, out_grad_late = lax.optimization_barrier((ffn, swapped, out_grad))
    w_ffn = lax.all_gather(ffn, ("x", "k"))
    grad_pieces = ygather(out_grad_late)
    half = zl.astype(jnp.int32)[None]
    results = mixer_call(half, sent, swapped, conv_weight, w_mixer)
    normed_one, inv_one = results[:2]
    proj, conv, before, acts, w_out = (results[i : i + 2] for i in range(2, 12, 2))

    out_parts, grad_pieces = lax.optimization_barrier((results[12:], grad_pieces))
    stream_own = block_in.astype(f32) + yreduce(out_parts)
    grads_own = jnp.concatenate(grad_pieces, axis=1)
    grads_other = zswap(grads_own)
    stream_sent = stream_own.astype(bf16)
    other = zswap(stream_sent)
    pieces_own = ygather(stream_sent)
    pieces_other = ygather(other)
    other_grads = [grads_other[:, 384 * j : 384 * j + 384] for j in range(4)]
    half_own = ffn_call(pieces_own, grad_pieces, gain_two, w_ffn)
    half_other = ffn_call(pieces_other, other_grads, gain_two, w_ffn, half_own[0])
    own_terms = yexchange(lambda j: half_own[4 + j])
    own_terms, half_other = lax.optimization_barrier((own_terms, half_other))
    other_terms = yexchange(lambda j: half_other[4 + j])
    normed_two = jnp.concatenate([half_own[0], half_other[0]], axis=0)
    theirs = t_dot(
        normed_two,
        jnp.concatenate(
            [jnp.where(k == 0, half[3], half[2]) for half in (half_own, half_other)], axis=0
        ),
    ).astype(bf16)
    hidden = jnp.concatenate([half_own[1], half_other[1]], axis=0)
    grads_all = jnp.concatenate([grads_own, grads_other], axis=0)
    down_grad = t_dot(grads_all, hidden)
    block_parts = block_call(half_own[1], half_other[1], w_ffn)
    other_terms, half_own, half_other, theirs, down_grad, block_parts = (
        lax.optimization_barrier(
            (other_terms, half_own, half_other, theirs, down_grad, block_parts)
        )
    )
    theirs = kswap(theirs)
    sum_other = total_of(other_terms)
    sum_own = total_of(own_terms)
    from_other = zswap(sum_other.astype(bf16))
    two_grad = sum_own + from_other.astype(f32)

    two_all = ygather(two_grad.astype(bf16))

    mine = t_dot(
        normed_two,
        jnp.concatenate(
            [jnp.where(k == 0, half[2], half[3]) for half in (half_own, half_other)], axis=0
        ),
    )
    gate_up_grad = (mine + theirs.astype(f32)).reshape(4, 4, 2, 48, FB)
    down_grad = split_k(down_grad.reshape(4, 2, 192, FB), k, 1).reshape(4, 4, 2, 24, FB)
    ffn = jnp.concatenate([gate_up_grad, down_grad], axis=3).astype(bf16)
    ffn = jnp.stack([pick(ffn, (b - y) % 4) for b in range(4)])
    ffn, two_all = lax.optimization_barrier((ffn, two_all))
    ffn = ffn.transpose(2, 1, 0, 3, 4).reshape(32, 72, FB)
    ffn = lax.all_to_all(ffn, ("zh", "x", "y"), 0, 0, tiled=True)

    stream_back, *grads, halo, own_stream_grad, gain_two_part = stream_call(
        two_all, pieces_own, grad_pieces, two_grad, gain_two, w_out, proj
    )
    halo = lax.ppermute(halo, "zl", [(1, 0)])
    results = back_call(
        sent, grads, proj, conv, before, halo, swapped, conv_weight, w_mixer
    )
    proj_back = results[:2]
    gain_one_part, *conv_parts = results[6:]
    one_parts = results[2:6]
    tails = []
    for r in range(2):
        taps_part = conv_parts[r].reshape(-1)
        rest = jnp.concatenate([taps_part[384:], jnp.zeros((192,), f32)])
        small = jnp.stack([gain_two_part[0], taps_part[:384], rest], axis=1)
        small = jnp.pad(small, ((0, D - 384), (577, 60)))
        small = small + jnp.pad(gain_one_part.T, ((0, 0), (576, 63)))
        padded = jnp.pad(acts[r], ((0, 0), (0, 64)))
        tails.append((t_dot(normed_one, proj_back[r]) + small, t_dot(stream_back, padded)))

    def tail_half(index):
        halves = []
        for pair in tails:
            rows = [
                lax.dynamic_index_in_dim(v.reshape(4, 2, 192, -1), index, 1, keepdims=False)
                for v in pair
            ]
            halves.append(jnp.concatenate(rows, axis=2))
        return jnp.stack(halves)

    theirs = tail_half(1 - k)
    one_terms = yexchange(lambda j: one_parts[j])
    theirs, ffn, one_terms, block_parts = lax.optimization_barrier(
        (theirs, ffn, one_terms, block_parts)
    )
    mixer = tail_half(k) + kswap(theirs.astype(bf16)).astype(f32)
    cols = list(jnp.sum(ffn.reshape(8, 4, 72, FB).astype(f32), axis=0).astype(bf16))
    part = jnp.concatenate(cols[:3] + [cols[3][:, 128:]], axis=1)
    part = gather_zh(part, zh)
    mixer = jnp.stack([pick(mixer.swapaxes(0, 1), (b - y) % 4) for b in range(4)])
    mixer = jnp.where(zl == 0, mixer, mixer[:, ::-1]).astype(bf16)
    mixer, part = lax.optimization_barrier((mixer, part))
    full = lax.all_gather(part, ("k", "x"))
    gate_up_out, down_out = ffn_finish(full)
    mixer = mixer.reshape(4, 2, 4, 2, 24, FB).transpose(3, 2, 1, 0, 4, 5)
    mixer = lax.all_to_all(
        mixer.reshape(64, 24, FB), ("zh", "x", "zl", "y"), 0, 0, tiled=True
    )
    block_terms = yexchange(lambda j: block_parts[j])
    one_sum = total_of(one_terms)
    one_grad = one_sum[:512]
    inner_one = one_sum[512:514].reshape(-1)[:512] + one_sum[514:516].reshape(-1)[:512]
    own_hat = block_in.astype(f32) * inv_one
    in_grad = own_stream_grad + inv_one * (
        gain_one[:, :384] * one_grad - own_hat * (inner_one / D)[:, None]
    )
    in_grad = in_grad.astype(bf16)
    cols = jnp.sum(mixer.reshape(16, 4, 24, FB).astype(f32), axis=0).astype(bf16)
    part = gather_zh(cols, zh)
    part, block_terms = lax.optimization_barrier((part, block_terms))
    block_sum = total_of(block_terms)
    from_other = zswap(block_sum[1].astype(bf16))
    from_other, gate_up_out, down_out = lax.optimization_barrier(
        (from_other, gate_up_out, down_out)
    )
    block_out = stream_own + block_sum[0] + from_other.astype(f32)
    block_out = block_out.astype(bf16)
    full = lax.all_gather(part, ("k", "x"))
    full, gate_up_out, down_out, in_grad, block_out = lax.optimization_barrier(
        (full, gate_up_out, down_out, in_grad, block_out)
    )
    in_out, out_out, own_small, sum_small = mixer_finish(full, y)
    gain_one_out = sum_small[:, 64]
    gain_two_out = own_small[:, 65]
    conv_out = jnp.concatenate([own_small[:, 66], own_small[:192, 67]]).reshape(3, 192)
    return (
        block_out,
        in_grad,
        gain_one_out,
        in_out,
        conv_out,
        out_out,
        gain_two_out,
        gate_up_out,
        down_out,
    )


def solution(mesh):
    devices = mesh.devices.reshape(2, 4, 2, 2, 4)
    grid = Mesh(devices, ("zh", "x", "k", "zl", "y"))
    tokens = P(("zh", "x", "k", "zl"), "y")
    first = P(None, "y", "zl")
    second = P("zl", "y")
    in_specs = (
        tokens,
        P("y"),
        first,
        P(None, ("zl", "y")),
        second,
        P("y"),
        first,
        second,
        tokens,
    )
    out_specs = (
        tokens,
        tokens,
        P("y"),
        first,
        P(None, ("zl", "y")),
        second,
        P("y"),
        first,
        second,
    )
    return jax.shard_map(body, mesh=grid, in_specs=in_specs, out_specs=out_specs, check_vma=False)
```

```python
import functools

import jax
import jax.numpy as jnp
from jax import lax
from jax.experimental import pallas as pl
from jax.experimental.pallas import tpu as pltpu
from jax.sharding import Mesh, PartitionSpec as P

D = 1536
LEN = 1024
EPSILON = 1e-05
FB = 896
FSTARTS = (0, 896, 1792, 2560)

bf16 = jnp.bfloat16
f32 = jnp.float32


def yshift(v, d):
    return lax.ppermute(v, "y", [(i, (i + d) % 4) for i in range(4)])


def xshift(v, d):
    return lax.ppermute(v, "x", [(i, (i + d) % 4) for i in range(4)])


def zshift(v, d):
    return lax.ppermute(v, ("zh", "zl"), [(i, (i + d) % 4) for i in range(4)])


def zswap(v):
    return lax.ppermute(v, "zl", [(0, 1), (1, 0)])


def kswap(v):
    return lax.ppermute(v, "k", [(0, 1), (1, 0)])


def ygather(v):
    two = yshift(v, 2)
    return [v, yshift(v, 3), two, yshift(v, 1)]


def yexchange(block_for):
    two = yshift(block_for(2), 2)
    one = yshift(block_for(1), 1)
    three = yshift(block_for(3), 3)
    return [block_for(0), three, two, one]


def yreduce(pieces):
    got = yexchange(lambda j: pieces[j].astype(bf16) if j else pieces[0])
    return got[0].astype(f32) + got[1].astype(f32) + got[2].astype(f32) + got[3].astype(f32)


def zexchange(v):
    half = v.shape[0] // 2
    up = zshift(v[:half], 1)
    down = zshift(v[half:], 3)
    return jnp.concatenate([up, down], axis=0)


def pick(stacked, index):
    return lax.dynamic_index_in_dim(stacked, index, 0, keepdims=False)


def dot(a, b):
    return jnp.dot(a, b, preferred_element_type=f32)


def dot_t(a, b):
    return lax.dot_general(a, b, (((1,), (1,)), ((), ())), preferred_element_type=f32)


def t_dot(a, b):
    return lax.dot_general(a, b, (((0,), (0,)), ((), ())), preferred_element_type=f32)


def after(v, *deps):
    for dep in deps:
        last = lax.slice(dep, [n - 1 for n in dep.shape], dep.shape).reshape(())
        v = v + (last * 0).astype(v.dtype)
    return v


def both(k, mine, other, axis):
    return jnp.where(
        k == 0,
        jnp.concatenate([mine, other], axis=axis),
        jnp.concatenate([other, mine], axis=axis),
    )


def to_owners(blocks, y):
    return jnp.stack(yexchange(lambda j: pick(blocks, (y + j) % 4)))


def pack_mixer(in_weight, out_weight, first):
    rows = lax.dynamic_slice_in_dim(in_weight, first, 48, axis=1)
    turned = lax.dynamic_slice_in_dim(out_weight.T, first, 48, axis=0)
    blocks = []
    for b in range(4):
        cols = slice(192 * b, 192 * b + 192)
        blocks.append(
            jnp.concatenate(
                [
                    rows[0, :, cols],
                    rows[1, :, cols],
                    rows[2, :, cols],
                    jnp.zeros((48, 64), bf16),
                    turned[:, cols],
                ],
                axis=1,
            )
        )
    return jnp.stack(blocks)


def pack_ffn(gate_up_weight, down_weight, first):
    rows = lax.dynamic_slice_in_dim(gate_up_weight, first, 48, axis=1)
    turned = lax.dynamic_slice_in_dim(down_weight.T, first, 48, axis=0)
    blocks = []
    for start in FSTARTS:
        cols = slice(start, start + FB)
        down = turned[:, cols]
        if start % FB:
            down = jnp.concatenate([jnp.zeros((48, 128), bf16), down[:, 128:]], axis=1)
        blocks.append(jnp.concatenate([rows[0, :, cols], rows[1, :, cols], down], axis=1))
    return jnp.stack(blocks)


def x_terms(pieces_of, x):
    got = [pieces_of(x)]
    for d in (2, 1, 3):
        got.append(xshift(pieces_of((x + d) % 4).astype(bf16), d))
    return got


def z_terms(own, other, zh, zl):
    z = 2 * zh + zl
    got = [pick(own, zh)]
    got.append(zshift(pick(own, 1 - zh).astype(bf16), 2))
    for d in (1, 3):
        got.append(zshift(pick(other, ((z + d) % 4) // 2).astype(bf16), d))
    return got


def zh_terms(v, axis, zh):
    mine = lax.dynamic_index_in_dim(v, zh, axis, keepdims=False)
    theirs = lax.dynamic_index_in_dim(v, 1 - zh, axis, keepdims=False).astype(bf16)
    return [mine, lax.ppermute(theirs, "zh", [(0, 1), (1, 0)])]


def total_of(terms):
    total = terms[0].astype(f32)
    for term in terms[1:]:
        total = total + term.astype(f32)
    return total


def to_columns(blocks, y):
    got = jnp.stack(yexchange(lambda j: blocks[j].astype(bf16)))
    return [pick(got, (b - y) % 4) for b in range(4)]


def gather_zh(part, zh):
    other = lax.ppermute(part, "zh", [(0, 1), (1, 0)])
    return jnp.where(zh == 0, jnp.stack([part, other]), jnp.stack([other, part]))


def split_k(v, k, axis):
    mine = lax.dynamic_index_in_dim(v, k, axis, keepdims=False)
    theirs = lax.dynamic_index_in_dim(v, 1 - k, axis, keepdims=False)
    return mine.astype(f32) + kswap(theirs.astype(bf16)).astype(f32)


TILES = ((0, 256), (256, 256), (512, 256), (768, 128))
CHEAP = pl.CostEstimate(flops=1_000_000, bytes_accessed=1_000_000, transcendentals=0)
WIDE = pltpu.CompilerParams(
    dimension_semantics=("arbitrary",), vmem_limit_bytes=50 * 1024 * 1024
)


def load_mixer(source, rows, sems):
    copies = []
    for r in range(2):
        for b in range(4):
            for e in range(8):
                first = 384 * b + 48 * e
                copies.append(
                    pltpu.make_async_copy(
                        source.at[e, r, b],
                        rows.at[r, pl.ds(first, 48)],
                        sems.at[32 * r + 8 * b + e],
                    )
                )
    for copy in copies:
        copy.start()
    for copy in copies:
        copy.wait()


def mixer_kernel(
    half_ref, x0, x1, x2, x3, swap_ref, taps_ref, w_hbm, n_ref, inv_ref, proj0, proj1,
    conv0, conv1, before0, before1, act0, act1, wo0, wo1, p0, p1, p2, p3, w_ref, sems,
):
    load_mixer(w_hbm, w_ref, sems)
    xs = (x0, x1, x2, x3)
    gain = jnp.concatenate([ref[512:528, :] for ref in xs], axis=1)[:1].astype(f32)
    for i in range(4):
        rows = pl.ds(128 * i, 128)
        wide = jnp.concatenate([ref[rows, :] for ref in xs], axis=1).astype(f32)
        inv = lax.rsqrt(jnp.sum(wide * wide, axis=1, keepdims=True) / D + EPSILON)
        inv_ref[rows, :] = inv
        n_ref[rows, :] = (wide * inv * gain).astype(bf16)
    tail = swap_ref[:16, :].astype(f32)
    tail = jnp.where(half_ref[0] == 1, tail, 0.0)
    inv = lax.rsqrt(jnp.sum(tail * tail, axis=1, keepdims=True) / D + EPSILON)
    n_tail = (tail * inv * gain).astype(bf16)
    own_taps = taps_ref[...].astype(f32)
    other_taps = swap_ref[16:32, :192].astype(f32)
    line = lax.broadcasted_iota(jnp.int32, (512, 192), 0)
    acts = (act0, act1)
    for r, taps in ((0, own_taps), (1, other_taps)):
        proj_ref = (proj0, proj1)[r]
        proj_ref[...] = dot(n_ref[...], w_ref[r, :, :576])
        proj_tail = dot(n_tail, w_ref[r, :, :576])
        before = proj_tail[8:, :192] * proj_tail[8:, 384:]
        (before0, before1)[r][...] = before
        mixed = proj_ref[:, :192] * proj_ref[:, 384:576]
        one = jnp.where(line == 0, before[7:8], pltpu.roll(mixed, 1, 0))
        two = jnp.where(
            line == 0, before[6:7], jnp.where(line == 1, before[7:8], pltpu.roll(mixed, 2, 0))
        )
        conv = taps[0:1] * mixed + taps[1:2] * one + taps[2:3] * two
        (conv0, conv1)[r][...] = conv
        acts[r][...] = (proj_ref[:, 192:384] * conv).astype(bf16)
        (wo0, wo1)[r][...] = w_ref[r, :, 640:]
    for j, ref in enumerate((p0, p1, p2, p3)):
        rows = pl.ds(384 * j, 384)
        part = dot_t(act0[...], wo0[rows, :]) + dot_t(act1[...], wo1[rows, :])
        ref[...] = part.astype(ref.dtype)


def mixer_call(half, pieces, swapped, taps, weight, *deps):
    whole = pl.BlockSpec(memory_space=pltpu.VMEM)

    def kernel(*refs):
        mixer_kernel(*refs[:8], *refs[8 + len(deps) :])

    def shape(*dims, kind=f32):
        return jax.ShapeDtypeStruct(dims, kind)

    return pl.pallas_call(
        kernel,
        in_specs=[pl.BlockSpec(memory_space=pltpu.SMEM)]
        + [whole] * 6
        + [pl.BlockSpec(memory_space=pl.ANY)] * (1 + len(deps)),
        out_specs=[whole] * 16,
        out_shape=[shape(512, D, kind=bf16), shape(512, 1)]
        + [shape(512, 576)] * 2
        + [shape(512, 192)] * 2
        + [shape(8, 192)] * 2
        + [shape(512, 192, kind=bf16)] * 2
        + [shape(D, 192, kind=bf16)] * 2
        + [shape(512, 384)]
        + [shape(512, 384, kind=bf16)] * 3,
        scratch_shapes=[pltpu.VMEM((2, D, 832), bf16), pltpu.SemaphoreType.DMA((64,))],
        compiler_params=pltpu.CompilerParams(vmem_limit_bytes=50 * 1024 * 1024),
        cost_estimate=CHEAP,
        name="mixer",
    )(half, *pieces, swapped, taps, weight, *deps)


def stream_kernel(*refs):
    q_refs, s_refs, g_refs = refs[:4], refs[4:8], refs[8:12]
    own_ref, gain_ref, wo0, wo1, proj0, proj1 = refs[12:18]
    sb_ref, grad0, grad1, halo_ref, sg_ref, gain_out = refs[-6:]
    gain = gain_ref[...]
    sums = jnp.zeros((1, 384), f32)
    for i in range(4):
        rows = pl.ds(128 * i, 128)
        stream = jnp.concatenate([ref[rows, :] for ref in s_refs], axis=1).astype(f32)
        inv = lax.rsqrt(jnp.sum(stream * stream, axis=1, keepdims=True) / D + EPSILON)
        hat = stream * inv
        weighted = gain * jnp.concatenate([ref[rows, :] for ref in q_refs], axis=1).astype(f32)
        mean = jnp.sum(weighted * hat, axis=1, keepdims=True) / D
        grads = jnp.concatenate([ref[rows, :] for ref in g_refs], axis=1).astype(f32)
        sb_ref[rows, :] = (grads + inv * (weighted - hat * mean)).astype(bf16)
        own = own_ref[rows, :]
        own_hat = hat[:, :384]
        sg_ref[rows, :] = grads[:, :384] + inv * (gain[:, :384] * own - own_hat * mean)
        sums = sums + jnp.sum(own * own_hat, axis=0, keepdims=True)
    gain_out[...] = sums
    for r in range(2):
        grad_ref = (grad0, grad1)[r]
        grad_ref[...] = dot(sb_ref[...], (wo0, wo1)[r][...])
        halo_ref[1 - r] = grad_ref[:8, :] * (proj0, proj1)[r][:8, 192:384]


def stream_call(two_all, streams, grads, two_grad, gain, w_out, proj, *deps):
    whole = pl.BlockSpec(memory_space=pltpu.VMEM)
    return pl.pallas_call(
        stream_kernel,
        in_specs=[whole] * 18 + [pl.BlockSpec(memory_space=pl.ANY)] * len(deps),
        out_specs=[whole] * 6,
        out_shape=[
            jax.ShapeDtypeStruct((512, D), bf16),
            jax.ShapeDtypeStruct((512, 192), f32),
            jax.ShapeDtypeStruct((512, 192), f32),
            jax.ShapeDtypeStruct((2, 8, 192), f32),
            jax.ShapeDtypeStruct((512, 384), f32),
            jax.ShapeDtypeStruct((1, 384), f32),
        ],
        compiler_params=pltpu.CompilerParams(vmem_limit_bytes=50 * 1024 * 1024),
        cost_estimate=CHEAP,
        name="stream",
    )(*two_all, *streams, *grads, two_grad, gain, *w_out, *proj, *deps)


def back_kernel(
    x0, x1, x2, x3, grad0, grad1, proj0, proj1, conv0, conv1, before0, before1, halo_ref,
    swap_ref, taps_ref, w_hbm, pb0, pb1, p0, p1, p2, p3, gain_out, taps0, taps1, w_ref, sems,
):
    load_mixer(w_hbm, w_ref, sems)
    xs = (x0, x1, x2, x3)
    own_taps = taps_ref[...].astype(f32)
    other_taps = swap_ref[16:32, :192].astype(f32)
    line = lax.broadcasted_iota(jnp.int32, (512, 192), 0)
    for r, taps in ((0, own_taps), (1, other_taps)):
        grad_ref, proj_ref = (grad0, grad1)[r], (proj0, proj1)[r]
        before, halo = (before0, before1)[r][...], halo_ref[r]
        grad = grad_ref[...]
        b_part = proj_ref[:, :192]
        x_part = proj_ref[:, 384:576]
        conv_back = grad * proj_ref[:, 192:384]
        one = jnp.where(line == 511, halo[0:1], pltpu.roll(conv_back, 511, 0))
        two = jnp.where(
            line == 510,
            halo[0:1],
            jnp.where(line == 511, halo[1:2], pltpu.roll(conv_back, 510, 0)),
        )
        mixed_grad = taps[0:1] * conv_back + taps[1:2] * one + taps[2:3] * two
        (pb0, pb1)[r][...] = jnp.concatenate(
            [
                mixed_grad * x_part,
                grad * (conv0, conv1)[r][...],
                mixed_grad * b_part,
                jnp.zeros((512, 64), f32),
            ],
            axis=1,
        ).astype(bf16)
        mixed = b_part * x_part
        lag_one = jnp.where(line == 0, before[7:8], pltpu.roll(mixed, 1, 0))
        lag_two = jnp.where(
            line == 0, before[6:7], jnp.where(line == 1, before[7:8], pltpu.roll(mixed, 2, 0))
        )
        (taps0, taps1)[r][...] = jnp.concatenate(
            [
                jnp.sum(conv_back * lagged, axis=0, keepdims=True)
                for lagged in (mixed, lag_one, lag_two)
            ],
            axis=0,
        )
    gain = jnp.concatenate([ref[512:528, :] for ref in xs], axis=1)[:1].astype(f32)
    ones = jnp.ones((8, D), bf16)
    inner = []
    sums = jnp.zeros((1, D), f32)
    for i in range(4):
        rows = pl.ds(128 * i, 128)
        part = dot_t(pb0[rows, :576], w_ref[0, :, :576]) + dot_t(
            pb1[rows, :576], w_ref[1, :, :576]
        )
        for j, ref in enumerate((p0, p1, p2, p3)):
            ref[rows, :] = part[:, 384 * j : 384 * j + 384].astype(ref.dtype)
        wide = jnp.concatenate([ref[rows, :] for ref in xs], axis=1).astype(f32)
        inv = lax.rsqrt(jnp.sum(wide * wide, axis=1, keepdims=True) / D + EPSILON)
        product = part * (wide * inv)
        sums = sums + jnp.sum(product, axis=0, keepdims=True)
        product = product * gain
        high = product.astype(bf16)
        low = (product - high.astype(f32)).astype(bf16)
        inner.append(dot_t(ones, high) + dot_t(ones, low))
    gain_out[...] = sums
    empty = jnp.zeros((1, 256), f32)
    rows = []
    total = jnp.concatenate(inner, axis=1)[:1]
    high = total.astype(bf16).astype(f32)
    for term in (high, total - high):
        rows.append(term[:, :384])
        rows.append(jnp.concatenate([term[:, 384:], empty], axis=1))
    inner_rows = jnp.concatenate(rows + [jnp.zeros((12, 384), f32)], axis=0)
    for ref in (p0, p1, p2, p3):
        ref[512:528, :] = inner_rows.astype(ref.dtype)


def back_call(pieces, grads, proj, conv, before, halo, swapped, taps, weight, *deps):
    whole = pl.BlockSpec(memory_space=pltpu.VMEM)

    def kernel(*refs):
        back_kernel(*refs[:16], *refs[16 + len(deps) :])

    return pl.pallas_call(
        kernel,
        in_specs=[whole] * 15 + [pl.BlockSpec(memory_space=pl.ANY)] * (1 + len(deps)),
        out_specs=[whole] * 9,
        out_shape=[jax.ShapeDtypeStruct((512, 640), bf16)] * 2
        + [jax.ShapeDtypeStruct((528, 384), f32)]
        + [jax.ShapeDtypeStruct((528, 384), bf16)] * 3
        + [jax.ShapeDtypeStruct((1, D), f32)]
        + [jax.ShapeDtypeStruct((3, 192), f32)] * 2,
        scratch_shapes=[pltpu.VMEM((2, D, 832), bf16), pltpu.SemaphoreType.DMA((64,))],
        compiler_params=pltpu.CompilerParams(vmem_limit_bytes=50 * 1024 * 1024),
        cost_estimate=CHEAP,
        name="back",
    )(*pieces, *grads, *proj, *conv, *before, halo, swapped, taps, weight, *deps)


def ffn_finish(full):
    def kernel(full_ref, gate_ref, down_ref):
        wide = full_ref[...].astype(f32)
        gate_ref[...] = wide[:, :, :48].reshape(2, 384, 384)
        down_ref[...] = wide[:, :, 48:].reshape(384, 384).T

    return pl.pallas_call(
        kernel,
        grid=(9,),
        in_specs=[pl.BlockSpec((8, 2, 72, 384), lambda i: (0, 0, 0, i))],
        out_specs=[
            pl.BlockSpec((2, 384, 384), lambda i: (0, 0, i)),
            pl.BlockSpec((384, 384), lambda i: (i, 0)),
        ],
        out_shape=[
            jax.ShapeDtypeStruct((2, 384, 3456), f32),
            jax.ShapeDtypeStruct((3456, 384), f32),
        ],
        compiler_params=pltpu.CompilerParams(vmem_limit_bytes=50 * 1024 * 1024),
        name="ffn_finish",
    )(full)


def mixer_finish(full, y):
    def kernel(y_ref, full_ref, in_ref, out_ref, own_ref, sum_ref):
        own = jnp.zeros((384, 128), f32)
        total = jnp.zeros((384, 128), f32)
        for b in range(4):
            block = full_ref[:, :, b].astype(f32).reshape(384, FB)
            cols = slice(192 * b, 192 * b + 192)
            for j in range(3):
                in_ref[j, :, cols] = block[:, 192 * j : 192 * j + 192]
            out_ref[cols, :] = block[:, 640:896].T[:192]
            small = block[:, 512:640]
            own = own + jnp.where(y_ref[0] == b, small, 0.0)
            total = total + small
        own_ref[...] = own
        sum_ref[...] = total

    whole = pl.BlockSpec(memory_space=pltpu.VMEM)
    return pl.pallas_call(
        kernel,
        in_specs=[pl.BlockSpec(memory_space=pltpu.SMEM), whole],
        out_specs=[whole] * 4,
        out_shape=[
            jax.ShapeDtypeStruct((3, 384, 768), f32),
            jax.ShapeDtypeStruct((768, 384), f32),
            jax.ShapeDtypeStruct((384, 128), f32),
            jax.ShapeDtypeStruct((384, 128), f32),
        ],
        compiler_params=pltpu.CompilerParams(vmem_limit_bytes=50 * 1024 * 1024),
        name="mixer_finish",
    )(y.astype(jnp.int32)[None], full)


def load_rows(source, rows, sems):
    copies = []
    for b in range(4):
        for e in range(8):
            first = 384 * b + 48 * e
            copies.append(
                pltpu.make_async_copy(
                    source.at[e, b], rows.at[pl.ds(first, 48)], sems.at[8 * b + e]
                )
            )
    for copy in copies:
        copy.start()
    for copy in copies:
        copy.wait()


def ffn_kernel(*refs):
    s_refs, g_refs = refs[:4], refs[4:8]
    gain_ref, w_hbm = refs[8:10]
    n_ref, h_ref, gb_ref, ub_ref = refs[-10:-6]
    p_refs = refs[-6:-2]
    w_ref, sems = refs[-2:]

    @pl.when(pl.program_id(0) == 0)
    def _():
        load_rows(w_hbm, w_ref, sems)

    stream = jnp.concatenate([ref[...] for ref in s_refs], axis=1).astype(f32)
    inv = lax.rsqrt(jnp.sum(stream * stream, axis=1, keepdims=True) / D + EPSILON)
    n_ref[...] = (stream * inv * gain_ref[...]).astype(bf16)
    grads = jnp.concatenate([ref[...] for ref in g_refs], axis=1)
    for first, size in TILES:
        cols = pl.ds(first, size)
        w_pair = jnp.concatenate(
            [w_ref[:, cols], w_ref[:, pl.ds(FB + first, size)]], axis=1
        )
        gate_up = dot(n_ref[...], w_pair)
        gate = gate_up[:, :size]
        up = gate_up[:, size:]
        sig = jax.nn.sigmoid(gate)
        silu = gate * sig
        h_ref[:, cols] = (silu * up).astype(bf16)
        hidden_grad = dot(grads, w_ref[:, pl.ds(2 * FB + first, size)])
        gb_ref[:, cols] = (
            hidden_grad * up * sig * (1.0 + gate * (1.0 - sig))
        ).astype(bf16)
        ub_ref[:, cols] = (hidden_grad * silu).astype(bf16)
    back = jnp.concatenate([gb_ref[...], ub_ref[...]], axis=1)
    parts = jnp.concatenate(
        [dot_t(back, w_ref[pl.ds(512 * i, 512), : 2 * FB]) for i in range(3)], axis=1
    )
    for j in range(4):
        p_refs[j][...] = parts[:, 384 * j : 384 * j + 384].astype(p_refs[j].dtype)


def ffn_call(streams, grads, gain, weight, *deps):
    narrow = pl.BlockSpec((256, 384), lambda i: (i, 0))
    middle = pl.BlockSpec((256, FB), lambda i: (i, 0))
    wide = pl.BlockSpec((256, D), lambda i: (i, 0))
    whole = pl.BlockSpec(memory_space=pl.ANY)
    return pl.pallas_call(
        ffn_kernel,
        grid=(2,),
        in_specs=[narrow] * 8
        + [pl.BlockSpec((1, D), lambda i: (0, 0)), whole]
        + [whole] * len(deps),
        out_specs=[wide] + [middle] * 3 + [narrow] * 4,
        out_shape=[jax.ShapeDtypeStruct((512, D), bf16)]
        + [jax.ShapeDtypeStruct((512, FB), bf16)] * 3
        + [jax.ShapeDtypeStruct((512, 384), f32)]
        + [jax.ShapeDtypeStruct((512, 384), bf16)] * 3,
        scratch_shapes=[pltpu.VMEM((D, 3 * FB), bf16), pltpu.SemaphoreType.DMA((32,))],
        compiler_params=WIDE,
        cost_estimate=pl.CostEstimate(
            flops=8_400_000_000, bytes_accessed=16_000_000, transcendentals=500_000
        ),
        name="ffn",
    )(*streams, *grads, gain, weight, *deps)


def block_kernel(h0_ref, h1_ref, w_ref, out_ref):
    hidden = jnp.where(pl.program_id(1) < 1, h0_ref[...], h1_ref[...])
    out_ref[0, 0] = dot_t(hidden, w_ref[...].reshape(384, FB)).astype(bf16)


def block_call(own, other, weight):
    def where(j, t):
        return (j, t, 0, 0)

    return pl.pallas_call(
        block_kernel,
        grid=(4, 2),
        in_specs=[
            pl.BlockSpec((512, FB), lambda j, t: (0, 0)),
            pl.BlockSpec((512, FB), lambda j, t: (0, 0)),
            pl.BlockSpec((8, None, 48, FB), lambda j, t: (0, j, 0, 2)),
        ],
        out_specs=pl.BlockSpec((1, 1, 512, 384), where),
        out_shape=jax.ShapeDtypeStruct((4, 2, 512, 384), bf16),
        compiler_params=pltpu.CompilerParams(vmem_limit_bytes=50 * 1024 * 1024),
        cost_estimate=pl.CostEstimate(
            flops=2_800_000_000, bytes_accessed=10_000_000, transcendentals=0
        ),
        name="block",
    )(own, other, weight)


def row_sum(v):
    return jnp.sum(v, axis=1, keepdims=True)


def body(
    block_in,
    norm_gain,
    in_weight,
    conv_weight,
    out_weight,
    ffn_gain,
    gate_up_weight,
    down_weight,
    out_grad,
):
    zh = lax.axis_index("zh")
    x = lax.axis_index("x")
    k = lax.axis_index("k")
    zl = lax.axis_index("zl")
    y = lax.axis_index("y")

    first = (2 * x + k) * 48
    mixer_own = to_owners(pack_mixer(in_weight, out_weight, first), y)
    sent = jnp.concatenate(
        [block_in, norm_gain[None], ffn_gain[None], jnp.zeros((14, 384), bf16)], axis=0
    )
    sent = ygather(sent)
    gain_one = jnp.concatenate([v[512:513] for v in sent], axis=1).astype(f32)
    gain_two = jnp.concatenate([v[513:514] for v in sent], axis=1).astype(f32)

    swapped = jnp.concatenate(
        [
            jnp.concatenate([v[496:512] for v in sent], axis=1),
            jnp.pad(conv_weight, ((0, 13), (0, D - 192))),
        ],
        axis=0,
    )
    swapped = zswap(swapped)

    mixer_both = jnp.stack([mixer_own, zexchange(mixer_own)])
    w_mixer = lax.all_gather(mixer_both, ("x", "k"))

    blocks = pack_ffn(gate_up_weight, down_weight, first)
    blocks, sent = lax.optimization_barrier((blocks, sent))
    ffn = to_owners(blocks, y)
    ffn, swapped, out_grad_late = lax.optimization_barrier((ffn, swapped, out_grad))
    w_ffn = lax.all_gather(ffn, ("x", "k"))
    grad_pieces = ygather(out_grad_late)
    half = zl.astype(jnp.int32)[None]
    results = mixer_call(half, sent, swapped, conv_weight, w_mixer)
    normed_one, inv_one = results[:2]
    proj, conv, before, acts, w_out = (results[i : i + 2] for i in range(2, 12, 2))

    out_parts, grad_pieces = lax.optimization_barrier((results[12:], grad_pieces))
    stream_own = block_in.astype(f32) + yreduce(out_parts)
    grads_own = jnp.concatenate(grad_pieces, axis=1)
    grads_other = zswap(grads_own)
    stream_sent = stream_own.astype(bf16)
    other = zswap(stream_sent)
    pieces_own = ygather(stream_sent)
    pieces_other = ygather(other)
    other_grads = [grads_other[:, 384 * j : 384 * j + 384] for j in range(4)]
    half_own = ffn_call(pieces_own, grad_pieces, gain_two, w_ffn)
    half_other = ffn_call(pieces_other, other_grads, gain_two, w_ffn, half_own[0])
    own_terms = yexchange(lambda j: half_own[4 + j])
    own_terms, half_other = lax.optimization_barrier((own_terms, half_other))
    other_terms = yexchange(lambda j: half_other[4 + j])
    normed_two = jnp.concatenate([half_own[0], half_other[0]], axis=0)
    theirs = t_dot(
        normed_two,
        jnp.concatenate(
            [jnp.where(k == 0, half[3], half[2]) for half in (half_own, half_other)], axis=0
        ),
    ).astype(bf16)
    hidden = jnp.concatenate([half_own[1], half_other[1]], axis=0)
    grads_all = jnp.concatenate([grads_own, grads_other], axis=0)
    down_grad = t_dot(grads_all, hidden)
    block_parts = block_call(half_own[1], half_other[1], w_ffn)
    other_terms, half_own, half_other, theirs, down_grad, block_parts = (
        lax.optimization_barrier(
            (other_terms, half_own, half_other, theirs, down_grad, block_parts)
        )
    )
    theirs = kswap(theirs)
    sum_other = total_of(other_terms)
    sum_own = total_of(own_terms)
    from_other = zswap(sum_other.astype(bf16))
    two_grad = sum_own + from_other.astype(f32)

    two_all = ygather(two_grad.astype(bf16))

    mine = t_dot(
        normed_two,
        jnp.concatenate(
            [jnp.where(k == 0, half[2], half[3]) for half in (half_own, half_other)], axis=0
        ),
    )
    gate_up_grad = (mine + theirs.astype(f32)).reshape(4, 4, 2, 48, FB)
    down_grad = split_k(down_grad.reshape(4, 2, 192, FB), k, 1).reshape(4, 4, 2, 24, FB)
    ffn = jnp.concatenate([gate_up_grad, down_grad], axis=3).astype(bf16)
    ffn = jnp.stack([pick(ffn, (b - y) % 4) for b in range(4)])
    ffn, two_all = lax.optimization_barrier((ffn, two_all))
    ffn = ffn.transpose(2, 1, 0, 3, 4).reshape(32, 72, FB)
    ffn = lax.all_to_all(ffn, ("zh", "x", "y"), 0, 0, tiled=True)

    stream_back, *grads, halo, own_stream_grad, gain_two_part = stream_call(
        two_all, pieces_own, grad_pieces, two_grad, gain_two, w_out, proj
    )
    halo = lax.ppermute(halo, "zl", [(1, 0)])
    results = back_call(
        sent, grads, proj, conv, before, halo, swapped, conv_weight, w_mixer
    )
    proj_back = results[:2]
    gain_one_part, *conv_parts = results[6:]
    one_parts = jnp.stack([v.astype(bf16) for v in results[2:6]])
    one_parts = jnp.stack([pick(one_parts, (b - y) % 4) for b in range(4)])
    one_sum = lax.psum_scatter(one_parts, "y", scatter_dimension=0, tiled=False)
    tails = []
    for r in range(2):
        taps_part = conv_parts[r].reshape(-1)
        rest = jnp.concatenate([taps_part[384:], jnp.zeros((192,), f32)])
        small = jnp.stack([gain_two_part[0], taps_part[:384], rest], axis=1)
        small = jnp.pad(small, ((0, D - 384), (577, 60)))
        small = small + jnp.pad(gain_one_part.T, ((0, 0), (576, 63)))
        padded = jnp.pad(acts[r], ((0, 0), (0, 64)))
        tails.append((t_dot(normed_one, proj_back[r]) + small, t_dot(stream_back, padded)))

    def tail_half(index):
        halves = []
        for pair in tails:
            rows = [
                lax.dynamic_index_in_dim(v.reshape(4, 2, 192, -1), index, 1, keepdims=False)
                for v in pair
            ]
            halves.append(jnp.concatenate(rows, axis=2))
        return jnp.stack(halves)

    theirs = tail_half(1 - k)
    theirs, ffn, block_parts = lax.optimization_barrier((theirs, ffn, block_parts))
    mixer = tail_half(k) + kswap(theirs.astype(bf16)).astype(f32)
    mixer, one_sum = lax.optimization_barrier((mixer, one_sum))
    cols = list(jnp.sum(ffn.reshape(8, 4, 72, FB).astype(f32), axis=0).astype(bf16))
    part = jnp.concatenate(cols[:3] + [cols[3][:, 128:]], axis=1)
    part = gather_zh(part, zh)
    mixer = jnp.stack([pick(mixer.swapaxes(0, 1), (b - y) % 4) for b in range(4)])
    mixer = jnp.where(zl == 0, mixer, mixer[:, ::-1]).astype(bf16)
    mixer, part = lax.optimization_barrier((mixer, part))
    full = lax.all_gather(part, ("k", "x"))
    gate_up_out, down_out = ffn_finish(full)
    mixer = mixer.reshape(4, 2, 4, 2, 24, FB).transpose(3, 2, 1, 0, 4, 5)
    mixer = lax.all_to_all(
        mixer.reshape(64, 24, FB), ("zh", "x", "zl", "y"), 0, 0, tiled=True
    )
    block_terms = yexchange(lambda j: block_parts[j])
    one_sum = one_sum.astype(f32)
    one_grad = one_sum[:512]
    inner_one = one_sum[512:514].reshape(-1)[:512] + one_sum[514:516].reshape(-1)[:512]
    own_hat = block_in.astype(f32) * inv_one
    in_grad = own_stream_grad + inv_one * (
        gain_one[:, :384] * one_grad - own_hat * (inner_one / D)[:, None]
    )
    in_grad = in_grad.astype(bf16)
    cols = jnp.sum(mixer.reshape(16, 4, 24, FB).astype(f32), axis=0).astype(bf16)
    part = gather_zh(cols, zh)
    part, block_terms = lax.optimization_barrier((part, block_terms))
    block_sum = total_of(block_terms)
    from_other = zswap(block_sum[1].astype(bf16))
    from_other, gate_up_out, down_out = lax.optimization_barrier(
        (from_other, gate_up_out, down_out)
    )
    block_out = stream_own + block_sum[0] + from_other.astype(f32)
    block_out = block_out.astype(bf16)
    full = lax.all_gather(part, ("k", "x"))
    full, gate_up_out, down_out, in_grad, block_out = lax.optimization_barrier(
        (full, gate_up_out, down_out, in_grad, block_out)
    )
    in_out, out_out, own_small, sum_small = mixer_finish(full, y)
    gain_one_out = sum_small[:, 64]
    gain_two_out = own_small[:, 65]
    conv_out = jnp.concatenate([own_small[:, 66], own_small[:192, 67]]).reshape(3, 192)
    return (
        block_out,
        in_grad,
        gain_one_out,
        in_out,
        conv_out,
        out_out,
        gain_two_out,
        gate_up_out,
        down_out,
    )


def solution(mesh):
    devices = mesh.devices.reshape(2, 4, 2, 2, 4)
    grid = Mesh(devices, ("zh", "x", "k", "zl", "y"))
    tokens = P(("zh", "x", "k", "zl"), "y")
    first = P(None, "y", "zl")
    second = P("zl", "y")
    in_specs = (
        tokens,
        P("y"),
        first,
        P(None, ("zl", "y")),
        second,
        P("y"),
        first,
        second,
        tokens,
    )
    out_specs = (
        tokens,
        tokens,
        P("y"),
        first,
        P(None, ("zl", "y")),
        second,
        P("y"),
        first,
        second,
    )
    return jax.shard_map(body, mesh=grid, in_specs=in_specs, out_specs=out_specs, check_vma=False)
```
